128 devices in a mesh: ctx: 2 (over core), dp: 64 (over z, y, x).
Axes of the slice: x: 4, y: 4, z: 4, core: 2. Of those that a mesh axis runs over, the one named last changes fastest.
Arguments:
- query_input: bfloat16 [64, 1024, 3072], P('dp', 'ctx'), may hold values from -6 to 6
- key_input: bfloat16 [64, 1024, 3072], P('dp', 'ctx'), may hold values from -6 to 6
- value_input: bfloat16 [64, 1024, 3072], P('dp', 'ctx'), may hold values from -6 to 6
- out_grad: bfloat16 [64, 1024, 3072], P('dp', 'ctx'), may hold values from -6 to 6
- log_decay: float32 [64, 24, 1024], P('dp', None, 'ctx'), may hold values from -1.5 to 0
- conv_kernel: float32 [3, 4, 3072], replicated, may hold values from -3 to 3
Outputs:
- query_grad: bfloat16 [64, 1024, 3072], P('dp', 'ctx')
- key_grad: bfloat16 [64, 1024, 3072], P('dp', 'ctx')
- value_grad: bfloat16 [64, 1024, 3072], P('dp', 'ctx')
- kernel_grad: float32 [3, 4, 3072], P(None, None, 'dp')
The draws below stay inside these ranges and needn't reach their ends.
All inputs are finite; a program needn't handle non-finite values.
Results may differ from the reference program's by a relative error of at most 0.0085.
Values may be sent and summed in bfloat16 or wider, within the bound.
A program may use at most 128 MiB of HBM per device.

```python
import jax
import jax.numpy as jnp
from jax import lax

LOCAL_HEADS = 24
DH = 128
KW = 4
BLK = 256
SEQ = 1024
HD = 3072
BATCH_SEQUENCES = 64


def draw_log_decay(key, part):
    key = jax.random.fold_in(key, 11)
    key_sequence = jax.random.split(key, 6)
    fast_share = 0.5
    chooser = jax.random.uniform(key_sequence[0], (1, LOCAL_HEADS, 1))
    fast_rate = jax.random.uniform(key_sequence[1], (1, LOCAL_HEADS, 1), minval=1.0 / 50.0, maxval=1.0 / 30.0)
    channel_attenuation = jnp.where(chooser < fast_share, fast_rate, 0.25 / SEQ)
    block_count = SEQ // BLK
    attenuation_multiplier = jnp.exp(jax.random.uniform(key_sequence[2], (BATCH_SEQUENCES, LOCAL_HEADS, block_count, 1), minval=-0.69, maxval=0.69))
    attenuation_multiplier = jnp.broadcast_to(attenuation_multiplier, (BATCH_SEQUENCES, LOCAL_HEADS, block_count, BLK)).reshape(BATCH_SEQUENCES, LOCAL_HEADS, SEQ)
    elementwise_multiple = jax.random.uniform(key_sequence[3], (BATCH_SEQUENCES, LOCAL_HEADS, SEQ), minval=0.5, maxval=1.5)
    timestep_ordinal = jax.random.randint(key_sequence[4], (BATCH_SEQUENCES, LOCAL_HEADS, 2, 1), 0, SEQ)
    segment_length = jax.random.uniform(key_sequence[5], (BATCH_SEQUENCES, LOCAL_HEADS, 2, 1), minval=0.22, maxval=0.69)
    placement_number = jnp.arange(SEQ)[None, None, None, :]
    segment_count = jnp.sum(jnp.where(placement_number == timestep_ordinal, segment_length, 0.0), axis=2)
    return (-(channel_attenuation * attenuation_multiplier * elementwise_multiple) - segment_count).astype(jnp.float32)


def shard_levels(stream_key, extent, cuts, least, largest):
    gain = 1.0
    for axis_at, shards_of in cuts:
        steps = jax.random.uniform(jax.random.fold_in(jax.random.fold_in(stream_key, 6), axis_at), (shards_of,), jnp.float32, least / len(cuts), largest / len(cuts))
        gain = gain * jnp.repeat(jnp.exp(steps), extent[axis_at] // shards_of).reshape((-1,) + (1,) * (len(extent) - 1 - axis_at))
    return gain


def normal_values(rng, shape, spread, bound, cuts=(), dtype=jnp.bfloat16):
    factor_of = shard_levels(rng, shape, cuts, -0.22, 0.18) if cuts else 1.0
    drawn = jax.random.normal(rng, shape, jnp.float32) * spread * factor_of
    return jnp.minimum(jnp.maximum(drawn, -bound), bound).astype(dtype)


def setup_inputs(seed: int = 0) -> dict:
    key_of = jax.random.split(jax.random.key(seed), 7)
    query_input = normal_values(key_of[0], (BATCH_SEQUENCES, SEQ, HD), 1.0, 6.0, ((0, 64), (1, 2)))
    key_input = normal_values(key_of[1], (BATCH_SEQUENCES, SEQ, HD), 1.0, 6.0, ((0, 64), (1, 2)))
    value_input = normal_values(key_of[2], (BATCH_SEQUENCES, SEQ, HD), 1.0, 6.0, ((0, 64), (1, 2)))
    out_grad = normal_values(key_of[3], (BATCH_SEQUENCES, SEQ, HD), 1.0, 6.0, ((0, 64), (1, 2)))
    log_decay = draw_log_decay(jax.random.fold_in(key_of[6], 71), 0)
    conv_kernel = normal_values(key_of[5], (3, KW, HD), KW ** -0.5, 3.0, (), jnp.float32)
    return dict(query_input=query_input, key_input=key_input, value_input=value_input, out_grad=out_grad, log_decay=log_decay, conv_kernel=conv_kernel)


def rounded(values):
    return lax.optimization_barrier(values.astype(jnp.bfloat16)).astype(jnp.float32)


def causal_conv(source, kernel):
    values = source.astype(jnp.float32)
    running = jnp.zeros(values.shape, jnp.float32)
    for offset in range(KW):
        shifted = jnp.pad(values, ((offset, 0), (0, 0)))[:SEQ]
        running = running + kernel[offset] * shifted
    return running


def transpose_conv(source, kernel):
    values = source.astype(jnp.float32)
    running = jnp.zeros(values.shape, jnp.float32)
    for offset in range(KW):
        shifted = jnp.pad(values, ((0, offset), (0, 0)))[offset:]
        running = running + kernel[offset] * shifted
    return running


def kernel_terms(source, gradient):
    values = source.astype(jnp.float32)
    grad_wide = gradient.astype(jnp.float32)
    rows_list = []
    for offset in range(KW):
        shifted = jnp.pad(values, ((offset, 0), (0, 0)))[:SEQ]
        rows_list.append(jnp.sum(shifted * grad_wide, axis=0))
    return jnp.stack(rows_list)


def block_grads(query_rows, rows_of_keys, rows_of_values, gradient_rows, local_sum, incoming, future_grads):
    scores_scale = 1.0 / DH
    totals = local_sum[:, -1:]
    key_matrix = jnp.exp(totals - local_sum).T[:, :, None]
    query_matrix = jnp.exp(local_sum).T[:, :, None]
    causal = jnp.arange(BLK)[:, None] >= jnp.arange(BLK)[None, :]
    differ = local_sum[:, :, None] - local_sum[:, None, :]
    mask_weight = jnp.where(causal, jnp.exp(jnp.where(causal, differ, 0.0)), 0.0)
    probabilities = rounded(jnp.einsum("thk,shk->hts", query_rows, rows_of_keys) * scores_scale * mask_weight)
    probability_grads = rounded(jnp.einsum("thv,shv->hts", gradient_rows, rows_of_values) * scores_scale * mask_weight)
    incoming_lower = rounded(incoming)
    future_lower = rounded(future_grads)
    query_change = jnp.einsum("oxi,ioy->xoy", probability_grads, rows_of_keys) + scores_scale * query_matrix * jnp.einsum("axm,xlm->axl", gradient_rows, incoming_lower)
    key_change = jnp.einsum("vpx,pvd->xvd", probability_grads, query_rows) + scores_scale * key_matrix * jnp.einsum("efl,fjl->efj", rows_of_values, future_lower)
    value_change = jnp.einsum("bea,ebm->abm", probabilities, gradient_rows) + scores_scale * key_matrix * jnp.einsum("dlj,ljc->dlc", rows_of_keys, future_lower)
    return (query_change.astype(jnp.bfloat16), key_change.astype(jnp.bfloat16), value_change.astype(jnp.bfloat16))


def one_sequence(items, conv_kernel):
    query_input, key_input, value_input, out_grad, log_decay = items
    blocks = SEQ // BLK
    conv_queries = causal_conv(query_input, conv_kernel[0]).astype(jnp.bfloat16)
    conv_keys = causal_conv(key_input, conv_kernel[1]).astype(jnp.bfloat16)
    conv_values = causal_conv(value_input, conv_kernel[2]).astype(jnp.bfloat16)
    query_rows = conv_queries.reshape(blocks, BLK, LOCAL_HEADS, DH).astype(jnp.float32)
    rows_of_keys = conv_keys.reshape(blocks, BLK, LOCAL_HEADS, DH).astype(jnp.float32)
    rows_of_values = conv_values.reshape(blocks, BLK, LOCAL_HEADS, DH).astype(jnp.float32)
    gradient_rows = out_grad.reshape(blocks, BLK, LOCAL_HEADS, DH).astype(jnp.float32)
    local_sum = jnp.cumsum(log_decay.reshape(LOCAL_HEADS, blocks, BLK), axis=2).transpose(1, 0, 2)
    totals = local_sum[:, :, -1]
    decays = jnp.exp(totals)
    key_matrix = jnp.exp(totals[:, :, None] - local_sum).transpose(0, 2, 1)[..., None]
    query_matrix = jnp.exp(local_sum).transpose(0, 2, 1)[..., None]
    weighted_keys = rounded(rows_of_keys * key_matrix)
    weighted_queries = rounded(query_rows * query_matrix)

    def forward_step(carried_state, inputs):
        block_of_keys, block_of_values, current_decay = inputs
        updated_state = current_decay[:, None, None] * carried_state + jnp.einsum("aif,aig->ifg", block_of_keys, block_of_values)
        return updated_state, carried_state

    zero_state = jnp.zeros((LOCAL_HEADS, DH, DH), jnp.float32)
    unused, incoming = lax.scan(forward_step, zero_state, (weighted_keys, rows_of_values, decays))

    def backward_step(future_grads, inputs):
        query_block, key_block, value_block, gradient_tile, sum_block, block_weighted, incoming_block, current_decay = inputs
        deltas = block_grads(query_block, key_block, value_block, gradient_tile, sum_block, incoming_block, future_grads)
        updated_state = jnp.einsum("mpl,mpf->plf", block_weighted, gradient_tile) + current_decay[:, None, None] * future_grads
        return updated_state, deltas

    unused_too, (query_change, key_change, value_change) = lax.scan(
        backward_step, zero_state,
        (query_rows, rows_of_keys, rows_of_values, gradient_rows, local_sum, weighted_queries, incoming, decays),
        reverse=True)
    query_change = query_change.reshape(SEQ, HD)
    key_change = key_change.reshape(SEQ, HD)
    value_change = value_change.reshape(SEQ, HD)
    query_grad = transpose_conv(query_change, conv_kernel[0]).astype(jnp.bfloat16)
    key_grad = transpose_conv(key_change, conv_kernel[1]).astype(jnp.bfloat16)
    value_grad = transpose_conv(value_change, conv_kernel[2]).astype(jnp.bfloat16)
    kernel_part = jnp.stack([kernel_terms(query_input, query_change), kernel_terms(key_input, key_change), kernel_terms(value_input, value_change)])
    return query_grad, key_grad, value_grad, kernel_part


def reference(query_input, key_input, value_input, out_grad, log_decay, conv_kernel):
    def per_sequence(items):
        return one_sequence(items, conv_kernel)

    query_grad, key_grad, value_grad, kernel_parts = lax.map(per_sequence, (query_input, key_input, value_input, out_grad, log_decay))
    return query_grad, key_grad, value_grad, jnp.sum(kernel_parts, axis=0) / BATCH_SEQUENCES
```

```python
import functools

import jax
import jax.numpy as jnp
from jax import lax
from jax.experimental import pallas as pl
from jax.experimental.pallas import tpu as pltpu
from jax.sharding import PartitionSpec as P

MESH = pl.DeviceIdType.MESH
BLK = 256
HALF = 128
LANES = 128
PAIR = 256
RIM = 16
CHUNK = 64
LOG2E = 1.4426950408889634
F32 = jnp.float32
BF16 = jnp.bfloat16
NT = (((1,), (1,)), ((), ()))
TN = (((0,), (0,)), ((), ()))
NN = (((1,), (0,)), ((), ()))


def dot(a, b, dims):
    return lax.dot_general(a, b, dims, preferred_element_type=F32)


def decay_tables(ld_ref, rows):
    upper = (
        lax.broadcasted_iota(jnp.int32, (BLK, BLK), 0)
        <= lax.broadcasted_iota(jnp.int32, (BLK, BLK), 1)
    ).astype(F32)
    heads, length = ld_ref.shape
    for b in range(length // BLK):
        span = slice(b * BLK, (b + 1) * BLK)
        sums = LOG2E * jnp.dot(
            ld_ref[:, span], upper, precision=lax.Precision.HIGHEST, preferred_element_type=F32
        )
        grown = jnp.exp2(sums)
        left = jnp.exp2(sums[:, BLK - 1 : BLK] - sums)
        for i in range(heads // 2):
            pair = slice(2 * i, 2 * i + 2)
            rows[i, :, span] = jnp.concatenate(
                [sums[pair], grown[pair], left[pair], jnp.zeros((2, BLK), F32)], axis=0
            )


def gradients_kernel(
    remote,
    q_any, k_any, v_any, q_ref, k_ref, v_ref, g_ref, ld_ref, w_ref,
    dq_ref, dk_ref, dv_ref, kg_ref,
    halo, xs, conv, scaled, rows, s_first, f_last, msg_out, msg_in,
    halo_send, halo_recv, msg_send, msg_recv,
):
    phase, i = pl.program_id(0), pl.program_id(1)
    steps = pl.num_programs(1)
    length = q_ref.shape[0]
    core = lax.axis_index("ctx") if remote else 0
    other = {"ctx": 1 - core}

    def halo_copy(m, source):
        return pltpu.make_async_remote_copy(
            src_ref=source.at[0, pl.ds(length - RIM, RIM), :],
            dst_ref=halo.at[m],
            send_sem=halo_send.at[m],
            recv_sem=halo_recv.at[m],
            device_id=other,
            device_id_type=MESH,
        )

    def state_copy(step):
        return pltpu.make_async_remote_copy(
            src_ref=msg_out.at[pl.ds(2 * step, 2)],
            dst_ref=msg_in.at[pl.ds(2 * step, 2)],
            send_sem=msg_send.at[step],
            recv_sem=msg_recv.at[step],
            device_id=other,
            device_id_type=MESH,
        )

    @pl.when((phase == 0) & (i == 0))
    def _():
        if remote:
            barrier = pltpu.get_barrier_semaphore()
            pl.semaphore_signal(barrier, inc=1, device_id=other, device_id_type=MESH)
            pl.semaphore_wait(barrier, 1)
            copies = [halo_copy(m, s) for m, s in enumerate((q_any, k_any, v_any))]
            for copy in copies:
                copy.start()
        decay_tables(ld_ref, rows)
        if remote:
            for copy in copies:
                copy.wait()
        else:
            halo[...] = jnp.zeros_like(halo)
            msg_in[...] = jnp.zeros_like(msg_in)

    @pl.when(phase == 0)
    def _():
        table = rows[i]
        columns = table.T
        for h in range(2):
            c = slice(h * LANES, (h + 1) * LANES)
            grown, left = columns[:, 2 + h : 3 + h], columns[:, 4 + h : 5 + h]
            for m, x_ref in enumerate((q_ref, k_ref, v_ref)):
                before = halo[m, :, pl.ds(pl.multiple_of(i * PAIR + h * LANES, LANES), LANES)]
                xs[i, h, m, 0:RIM] = jnp.where(core == 1, before.astype(F32), 0.0)
                for r in range(0, length, CHUNK):
                    xs[i, h, m, RIM + r : RIM + r + CHUNK] = x_ref[r : r + CHUNK, c].astype(F32)
                taps = [w_ref[m, j : j + 1, c] for j in range(4)]
                for r in range(0, length, CHUNK):
                    part = slice(r, r + CHUNK)
                    acc = taps[0] * xs[i, h, m, RIM + r : RIM + r + CHUNK]
                    for j in range(1, 4):
                        acc = acc + taps[j] * xs[i, h, m, RIM + r - j : RIM + r - j + CHUNK]
                    conv[m, i, part, c] = acc.astype(BF16)
                    if m > 0:
                        scaled[m, i, part, c] = (acc * left[part]).astype(BF16)
            for r in range(0, length, CHUNK):
                part = slice(r, r + CHUNK)
                scaled[0, i, part, c] = (g_ref[part, c].astype(F32) * grown[part]).astype(BF16)
            states, futures = [], []
            for b in range(2):
                part = slice(b * BLK, (b + 1) * BLK)
                states.append(dot(conv[1, i, part, c], scaled[2, i, part, c], TN))
                futures.append(dot(conv[0, i, part, c], scaled[0, i, part, c], TN))
            decay = [table[2 + h : 3 + h, (b + 1) * BLK - 1 : (b + 1) * BLK] for b in range(2)]
            s_first[2 * i + h] = states[0]
            f_last[2 * i + h] = futures[1]
            msg_out[2 * i + h] = jnp.where(
                core == 0, states[1] + decay[1] * states[0], futures[0] + decay[0] * futures[1]
            ).astype(BF16)
        if remote:
            state_copy(i).start()

    @pl.when(phase == 1)
    def _():
        if remote:
            state_copy(i).wait()
        table = rows[i]
        columns = table.T
        scale = 1.0 / LANES
        causal = lax.broadcasted_iota(jnp.int32, (HALF, HALF), 0) <= lax.broadcasted_iota(
            jnp.int32, (HALF, HALF), 1
        )
        for h in range(2):
            c = slice(h * LANES, (h + 1) * LANES)
            decay = [table[2 + h : 3 + h, (b + 1) * BLK - 1 : (b + 1) * BLK] for b in range(2)]
            message = msg_in[2 * i + h].astype(F32) * scale
            state_in = jnp.where(core == 1, message, 0.0)
            future_in = jnp.where(core == 0, message, 0.0)
            incoming = [state_in, decay[0] * state_in + scale * s_first[2 * i + h]]
            future = [decay[1] * future_in + scale * f_last[2 * i + h], future_in]
            kernel_sums = [[jnp.zeros((8, LANES), F32) for _ in range(4)] for _ in range(3)]
            for b in range(2):
                part = slice(b * BLK, (b + 1) * BLK)
                q, k, v = (conv[m, i, part, c] for m in range(3))
                wg, wk, wv = (scaled[m, i, part, c] for m in range(3))
                g = g_ref[part, c]
                before = incoming[b].astype(BF16)
                after = future[b].astype(BF16)
                row = table[h : h + 1, part] - 7.0
                column = columns[part, h : h + 1]

                def weight(s, t):
                    mine = jnp.exp2(
                        row[:, t * HALF : (t + 1) * HALF] - column[s * HALF : (s + 1) * HALF]
                    )
                    return jnp.where(causal, mine, 0.0) if s == t else mine

                top = jnp.concatenate([weight(0, 0), weight(0, 1)], axis=1)
                low = weight(1, 1)
                pt_top = (dot(k[:HALF], q, NT) * top).astype(BF16)
                pt_low = (dot(k[HALF:], q[HALF:], NT) * low).astype(BF16)
                gt_top = (dot(v[:HALF], g, NT) * top).astype(BF16)
                gt_low = (dot(v[HALF:], g[HALF:], NT) * low).astype(BF16)
                dk_far = dot(wv, after, NT)
                dv_far = dot(wk, after, NN)
                dq_far = dot(wg, before, NT)
                dk = [dot(gt_top, q, NN) + dk_far[:HALF], dot(gt_low, q[HALF:], NN) + dk_far[HALF:]]
                dv = [dot(pt_top, g, NN) + dv_far[:HALF], dot(pt_low, g[HALF:], NN) + dv_far[HALF:]]
                dq_near = dot(gt_top, k[:HALF], TN)
                dq = [
                    dq_near[:HALF] + dq_far[:HALF],
                    dq_near[HALF:] + dot(gt_low, k[HALF:], TN) + dq_far[HALF:],
                ]
                for m, (grads, ref) in enumerate(((dq, dq_ref), (dk, dk_ref), (dv, dv_ref))):
                    for half in range(2):
                        base = b * BLK + half * HALF
                        ref[base : base + HALF, c] = grads[half].astype(BF16)
                        for j in range(4):
                            shifted = xs[i, h, m, RIM + base - j : RIM + base - j + HALF]
                            terms = (shifted * grads[half]).reshape(HALF // 8, 8, LANES)
                            kernel_sums[m][j] = kernel_sums[m][j] + jnp.sum(terms, axis=0)
            kg_ref[:, c] = jnp.concatenate(
                [jnp.sum(kernel_sums[m][j], axis=0, keepdims=True) for m in range(3) for j in range(4)]
                + [jnp.zeros((4, LANES), F32)],
                axis=0,
            )


def gradients(query, key, value, out_grad, log_decay, conv_kernel, remote=True):
    _, length, width = query.shape
    heads = log_decay.shape[1]
    steps = width // PAIR
    first = lambda p, i: (0, 0, i * (1 - p) + (steps - 1) * p)
    both = lambda p, i: (0, 0, i)
    late = lambda p, i: (0, i * p)
    block = pl.BlockSpec((None, length, PAIR), first)
    out_block = pl.BlockSpec((length, PAIR), late)
    return pl.pallas_call(
        functools.partial(gradients_kernel, remote),
        grid=(2, steps),
        in_specs=[pl.BlockSpec(memory_space=pl.ANY)] * 3
        + [block] * 3
        + [
            pl.BlockSpec((None, length, PAIR), both),
            pl.BlockSpec((None, heads, length), lambda p, i: (0, 0, 0)),
            pl.BlockSpec((3, 4, PAIR), first),
        ],
        out_specs=[out_block] * 3 + [pl.BlockSpec((16, PAIR), late)],
        out_shape=[jax.ShapeDtypeStruct((length, width), BF16)] * 3
        + [jax.ShapeDtypeStruct((16, width), F32)],
        scratch_shapes=[
            pltpu.VMEM((3, RIM, width), BF16),
            pltpu.VMEM((steps, 2, 3, RIM + length, LANES), F32),
            pltpu.VMEM((3, steps, length, PAIR), BF16),
            pltpu.VMEM((3, steps, length, PAIR), BF16),
            pltpu.VMEM((steps, 8, length), F32),
            pltpu.VMEM((heads, LANES, LANES), F32),
            pltpu.VMEM((heads, LANES, LANES), F32),
            pltpu.VMEM((heads, LANES, LANES), BF16),
            pltpu.VMEM((heads, LANES, LANES), BF16),
            pltpu.SemaphoreType.DMA((3,)),
            pltpu.SemaphoreType.DMA((3,)),
            pltpu.SemaphoreType.DMA((steps,)),
            pltpu.SemaphoreType.DMA((steps,)),
        ],
        compiler_params=pltpu.CompilerParams(
            collective_id=0 if remote else None,
            has_side_effects=True,
            dimension_semantics=("arbitrary", "arbitrary"),
            vmem_limit_bytes=60 * 1024 * 1024,
        ),
        name="gradients",
    )(query, key, value, query, key, value, out_grad, log_decay, conv_kernel)


def reduce_kernel(
    dq_any, dk_any, dv_any, kg_ref,
    after_ref, out_ref,
    z_in, y_src, y_in, x_src, x_in,
    halo_send, halo_recv, z_send, z_recv, y_send, y_recv, x_send, x_recv,
):
    core, dp = lax.axis_index("ctx"), lax.axis_index("dp")
    z, y, x = dp // 16, lax.rem(dp // 4, 4), lax.rem(dp, 4)
    width = kg_ref.shape[1]
    z_width, y_width, x_width = width // 4, width // 16, width // 64

    def device(c, zz, yy, xx):
        return {"ctx": c, "dp": zz * 16 + yy * 4 + xx}

    def turned(value, by):
        return lax.rem(value + by, 4)

    z_peers = [(d, device(core, turned(z, d), y, x)) for d in range(1, 4)]
    y_peers = [(d, device(core, z, turned(y, d), x)) for d in range(1, 4)]
    x_peers = [
        (4 * e + d, device(core if e == 0 else 1 - core, z, y, turned(x, d)))
        for e in range(2)
        for d in range(4)
        if e + d > 0
    ]
    barrier = pltpu.get_barrier_semaphore()
    everyone = z_peers + y_peers + x_peers
    for _, peer in everyone:
        pl.semaphore_signal(barrier, inc=1, device_id=peer, device_id_type=MESH)
    pl.semaphore_wait(barrier, len(everyone))

    def send(source, target, send_sem, recv_sem, peer):
        copy = pltpu.make_async_remote_copy(
            src_ref=source, dst_ref=target, send_sem=send_sem, recv_sem=recv_sem,
            device_id=peer, device_id_type=MESH,
        )
        copy.start()
        return copy

    z_copies = [
        send(
            kg_ref.at[:, pl.ds(pl.multiple_of(turned(z, d) * z_width, LANES), z_width)],
            z_in.at[d - 1], z_send.at[d - 1], z_recv.at[d - 1], peer,
        )
        for d, peer in z_peers
    ]
    halo_copies = [
        send(
            source.at[pl.ds(0, RIM), :], after_ref.at[m], halo_send.at[m], halo_recv.at[m],
            device(1 - core, z, y, x),
        )
        for m, source in enumerate((dq_any, dk_any, dv_any))
    ]
    total = kg_ref[:, pl.ds(pl.multiple_of(z * z_width, LANES), z_width)]
    for d, copy in enumerate(z_copies):
        copy.wait()
        total = total + z_in[d]
    for p in range(4):
        y_src[p] = jnp.concatenate(
            [total[:, p * y_width : (p + 1) * y_width], jnp.zeros((16, 256 - y_width), F32)], axis=1
        )
    y_copies = [
        send(y_src.at[turned(y, d)], y_in.at[d - 1], y_send.at[d - 1], y_recv.at[d - 1], peer)
        for d, peer in y_peers
    ]
    total = y_src[y]
    for d, copy in enumerate(y_copies):
        copy.wait()
        total = total + y_in[d]
    for p in range(4):
        x_src[p] = jnp.concatenate(
            [total[:, p * x_width : (p + 1) * x_width], jnp.zeros((16, 128 - x_width), F32)], axis=1
        )
    x_copies = [
        send(x_src.at[turned(x, s % 4)], x_in.at[s - 1], x_send.at[s - 1], x_recv.at[s - 1], peer)
        for s, peer in x_peers
    ]
    total = x_src[x]
    for s, copy in enumerate(x_copies):
        copy.wait()
        total = total + x_in[s]
    total = total * (1.0 / 64)
    for m in range(3):
        out_ref[m] = total[4 * m : 4 * m + 4, :x_width]
    for copy in halo_copies:
        copy.wait()


def reduce_terms(dq, dk, dv, kg):
    width = dq.shape[1]
    dma = pltpu.SemaphoreType.DMA
    return pl.pallas_call(
        reduce_kernel,
        in_specs=[pl.BlockSpec(memory_space=pl.ANY)] * 3 + [pl.BlockSpec(memory_space=pltpu.VMEM)],
        out_specs=[pl.BlockSpec(memory_space=pltpu.VMEM)] * 2,
        out_shape=[
            jax.ShapeDtypeStruct((3, RIM, width), BF16),
            jax.ShapeDtypeStruct((3, 4, width // 64), F32),
        ],
        scratch_shapes=[
            pltpu.VMEM((3, 16, width // 4), F32),
            pltpu.VMEM((4, 16, 256), F32),
            pltpu.VMEM((3, 16, 256), F32),
            pltpu.VMEM((4, 16, 128), F32),
            pltpu.VMEM((7, 16, 128), F32),
            dma((3,)), dma((3,)), dma((3,)), dma((3,)), dma((3,)), dma((3,)), dma((7,)), dma((7,)),
        ],
        compiler_params=pltpu.CompilerParams(collective_id=1, has_side_effects=True),
        name="reduce_terms",
    )(dq, dk, dv, kg)


def spread_kernel(dq_ref, dk_ref, dv_ref, after_ref, w_ref, oq_ref, ok_ref, ov_ref, wide):
    core = lax.axis_index("ctx")
    length = dq_ref.shape[0]
    for m, (ref, out) in enumerate(((dq_ref, oq_ref), (dk_ref, ok_ref), (dv_ref, ov_ref))):
        for h in range(2):
            c = slice(h * LANES, (h + 1) * LANES)
            for r in range(0, length, CHUNK):
                wide[m, h, r : r + CHUNK] = ref[r : r + CHUNK, c].astype(F32)
            wide[m, h, length : length + RIM] = jnp.where(
                core == 0, after_ref[m, :, c].astype(F32), 0.0
            )
            taps = [w_ref[m, j : j + 1, c] for j in range(4)]
            for r in range(0, length, CHUNK):
                acc = taps[0] * wide[m, h, r : r + CHUNK]
                for j in range(1, 4):
                    acc = acc + taps[j] * wide[m, h, r + j : r + j + CHUNK]
                out[r : r + CHUNK, c] = acc.astype(BF16)


def spread(dq, dk, dv, after, conv_kernel):
    length, width = dq.shape
    column = lambda i: (0, i)
    return pl.pallas_call(
        spread_kernel,
        grid=(width // PAIR,),
        in_specs=[pl.BlockSpec((length, PAIR), column)] * 3
        + [
            pl.BlockSpec((3, RIM, PAIR), lambda i: (0, 0, i)),
            pl.BlockSpec((3, 4, PAIR), lambda i: (0, 0, i)),
        ],
        out_specs=[pl.BlockSpec((None, length, PAIR), lambda i: (0, 0, i))] * 3,
        out_shape=[jax.ShapeDtypeStruct((1, length, width), BF16)] * 3,
        scratch_shapes=[pltpu.VMEM((3, 2, length + RIM, LANES), F32)],
        compiler_params=pltpu.CompilerParams(dimension_semantics=("arbitrary",)),
        name="spread",
    )(dq, dk, dv, after, conv_kernel)


def local(query, key, value, out_grad, log_decay, conv_kernel):
    dq, dk, dv, kg = gradients(query, key, value, out_grad, log_decay, conv_kernel)
    after, kernel_grad = reduce_terms(dq, dk, dv, kg)
    outputs = spread(dq, dk, dv, after, conv_kernel)
    return (*outputs, kernel_grad)


def solution(mesh):
    rows = P("dp", "ctx", None)
    return jax.shard_map(
        local,
        mesh=mesh,
        in_specs=(rows, rows, rows, rows, P("dp", None, "ctx"), P()),
        out_specs=(rows, rows, rows, P(None, None, "dp")),
        check_vma=False,
    )
```

```python
import functools

import jax
import jax.numpy as jnp
from jax import lax
from jax.experimental import pallas as pl
from jax.experimental.pallas import tpu as pltpu
from jax.sharding import PartitionSpec as P

MESH = pl.DeviceIdType.MESH
BLK = 256
HALF = 128
LANES = 128
PAIR = 256
RIM = 16
CHUNK = 64
PIECES = ((0, 5), (5, 10), (10, 16))
LOG2E = 1.4426950408889634
F32 = jnp.float32
BF16 = jnp.bfloat16
NT = (((1,), (1,)), ((), ()))
TN = (((0,), (0,)), ((), ()))
NN = (((1,), (0,)), ((), ()))


def dot(a, b, dims):
    return lax.dot_general(a, b, dims, preferred_element_type=F32)


def decay_tables(ld_ref, rows):
    upper = (
        lax.broadcasted_iota(jnp.int32, (BLK, BLK), 0)
        <= lax.broadcasted_iota(jnp.int32, (BLK, BLK), 1)
    ).astype(F32)
    heads, length = ld_ref.shape
    for b in range(length // BLK):
        span = slice(b * BLK, (b + 1) * BLK)
        sums = LOG2E * jnp.dot(
            ld_ref[:, span], upper, precision=lax.Precision.HIGHEST, preferred_element_type=F32
        )
        grown = jnp.exp2(sums)
        left = jnp.exp2(sums[:, BLK - 1 : BLK] - sums)
        for i in range(heads // 2):
            pair = slice(2 * i, 2 * i + 2)
            rows[i, :, span] = jnp.concatenate(
                [sums[pair], grown[pair], left[pair], jnp.zeros((2, BLK), F32)], axis=0
            )


def down(row):
    return jnp.broadcast_to(row, (LANES, LANES)).T


def diagonal(a, b):
    zero = jnp.zeros_like(a)
    return jnp.concatenate(
        [jnp.concatenate([a, zero], axis=1), jnp.concatenate([zero, b], axis=1)], axis=0
    )


def rim_kernel(q_any, k_any, v_any, halo_any, send_sem, recv_sem):
    length = q_any.shape[1]
    other = {"ctx": 1 - lax.axis_index("ctx")}
    barrier = pltpu.get_barrier_semaphore()
    pl.semaphore_signal(barrier, inc=1, device_id=other, device_id_type=MESH)
    pl.semaphore_wait(barrier, 1)
    copies = [
        pltpu.make_async_remote_copy(
            src_ref=source.at[0, pl.ds(length - RIM, RIM), :],
            dst_ref=halo_any.at[m],
            send_sem=send_sem.at[m],
            recv_sem=recv_sem.at[m],
            device_id=other,
            device_id_type=MESH,
        )
        for m, source in enumerate((q_any, k_any, v_any))
    ]
    for copy in copies:
        copy.start()
    for copy in copies:
        copy.wait()


def rims(query, key, value):
    return pl.pallas_call(
        rim_kernel,
        in_specs=[pl.BlockSpec(memory_space=pl.ANY)] * 3,
        out_specs=pl.BlockSpec(memory_space=pl.ANY),
        out_shape=jax.ShapeDtypeStruct((3, RIM, query.shape[2]), BF16),
        scratch_shapes=[pltpu.SemaphoreType.DMA((3,)), pltpu.SemaphoreType.DMA((3,))],
        compiler_params=pltpu.CompilerParams(collective_id=0, has_side_effects=True),
        name="rims",
    )(query, key, value)


def main_kernel(
    remote,
    q_any, k_any, v_any, g_any, halo_ref, ld_ref, w_ref,
    oq_any, ok_any, ov_any, kernel_grad_ref,
    xs, store, scaled, rows, s_first, f_last, msg_out, msg_in,
    terms, pieces, landed, part_out, part_in,
    in_sem, out_sem, msg_send, msg_recv, rim_send, rim_recv, piece_send, piece_recv, part_send,
    part_recv,
):
    steps, _, length, _ = store.shape
    core = lax.axis_index("ctx") if remote else 0
    dp = lax.axis_index("dp") if remote else 0
    peers = pieces.shape[0]
    other = {"ctx": 1 - core}
    share = terms.shape[1] // peers

    def columns(i, h=0, width=PAIR):
        return pl.ds(pl.multiple_of(i * PAIR + h * LANES, LANES), width)

    def fetch(i, m):
        source = (q_any, k_any, v_any, g_any)[m]
        return pltpu.make_async_copy(source.at[0, :, columns(i)], store.at[i, m], in_sem.at[i, m])

    def flush(i, m):
        target = (oq_any, ok_any, ov_any)[m]
        return pltpu.make_async_copy(store.at[i, m], target.at[0, :, columns(i)], out_sem.at[i, m])

    def remote_copy(source, target, send_sem, recv_sem, device):
        return pltpu.make_async_remote_copy(
            src_ref=source, dst_ref=target, send_sem=send_sem, recv_sem=recv_sem,
            device_id=device, device_id_type=MESH,
        )

    def state_copy(i):
        pair = pl.ds(2 * i, 2)
        return remote_copy(msg_out.at[pair], msg_in.at[pair], msg_send.at[i], msg_recv.at[i], other)

    def rim_copy(i):
        return remote_copy(
            xs.at[i, :, :, pl.ds(RIM, 8), :], xs.at[i, :, :, pl.ds(RIM + length, 8), :],
            rim_send.at[i], rim_recv.at[i], other,
        )

    def loop(count, body):
        def step(i, carry):
            body(i)
            return carry

        lax.fori_loop(0, count, step, 0)

    @functools.partial(loop, steps)
    def _(i):
        for m in range(4):
            fetch(i, m).start()

    if remote:
        barrier = pltpu.get_barrier_semaphore()
        pl.semaphore_signal(barrier, inc=1, device_id=other, device_id_type=MESH)

        @functools.partial(loop, peers - 1)
        def _(d):
            peer = {"dp": lax.rem(dp + d + 1, peers)}
            pl.semaphore_signal(barrier, inc=1, device_id=peer, device_id_type=MESH)
    else:
        msg_in[...] = jnp.zeros_like(msg_in)

    decay_tables(ld_ref, rows)

    @functools.partial(loop, steps)
    def _(i):
        for m in range(4):
            fetch(i, m).wait()
        table = rows[i]
        for h in range(2):
            c = slice(h * LANES, (h + 1) * LANES)
            for m in range(3):
                before = halo_ref[m, :, columns(i, h, LANES)].astype(F32)
                xs[i, h, m, 0:RIM] = jnp.where(core == 1, before, 0.0)
                for r in range(0, length, CHUNK):
                    xs[i, h, m, RIM + r : RIM + r + CHUNK] = store[i, m, r : r + CHUNK, c].astype(F32)
            taps = [[w_ref[m, j : j + 1, columns(i, h, LANES)] for j in range(4)] for m in range(3)]
            for base in range(0, length, LANES):
                grown = down(table[2 + h : 3 + h, base : base + LANES])
                left = down(table[4 + h : 5 + h, base : base + LANES])
                for r in range(0, LANES, CHUNK):
                    part = slice(base + r, base + r + CHUNK)
                    near = slice(r, r + CHUNK)
                    for m in range(3):
                        at = RIM + base + r
                        acc = taps[m][0] * xs[i, h, m, at : at + CHUNK]
                        for j in range(1, 4):
                            acc = acc + taps[m][j] * xs[i, h, m, at - j : at - j + CHUNK]
                        store[i, m, part, c] = acc.astype(BF16)
                        if m > 0:
                            scaled[m, i, part, c] = (acc * left[near]).astype(BF16)
                    scaled[0, i, part, c] = (store[i, 3, part, c].astype(F32) * grown[near]).astype(BF16)
        first, last = pl.ds(0, BLK), pl.ds(BLK, BLK)
        own = pl.ds(pl.multiple_of((1 - core) * BLK, BLK), BLK)
        state = dot(store[i, 1, first, :], scaled[2, i, first, :], TN)
        future = dot(store[i, 0, last, :], scaled[0, i, last, :], TN)
        message = dot(store[i, 1 - core, own, :], scaled[2 - 2 * core, i, own, :], TN)
        for h in range(2):
            c = slice(h * LANES, (h + 1) * LANES)
            decay = [table[2 + h : 3 + h, (b + 1) * BLK - 1 : (b + 1) * BLK] for b in range(2)]
            s_first[2 * i + h] = state[c, c]
            f_last[2 * i + h] = future[c, c]
            msg_out[2 * i + h] = (
                message[c, c]
                + jnp.where(core == 0, decay[1] * state[c, c], decay[0] * future[c, c])
            ).astype(BF16)
        if remote:

            @pl.when(i == steps - 2)
            def _():
                pl.semaphore_wait(pltpu.get_barrier_semaphore(), peers)
                loop(steps - 1, lambda n: state_copy(n).start())

            @pl.when(i == steps - 1)
            def _():
                state_copy(steps - 1).start()

    @functools.partial(loop, steps)
    def _(i):
        if remote:
            state_copy(i).wait()
        table = rows[i]
        scale = 1.0 / LANES
        causal = lax.broadcasted_iota(jnp.int32, (HALF, HALF), 0) <= lax.broadcasted_iota(
            jnp.int32, (HALF, HALF), 1
        )
        blank = jnp.zeros((HALF, HALF), BF16)
        incoming, future = [], []
        for h in range(2):
            decay = [table[2 + h : 3 + h, (b + 1) * BLK - 1 : (b + 1) * BLK] for b in range(2)]
            message = msg_in[2 * i + h].astype(F32) * scale
            state_in = jnp.where(core == 1, message, 0.0)
            future_in = jnp.where(core == 0, message, 0.0)
            state = decay[0] * state_in + scale * s_first[2 * i + h]
            grads = decay[1] * future_in + scale * f_last[2 * i + h]
            incoming.append([state_in.astype(BF16), state.astype(BF16)])
            future.append([grads.astype(BF16), future_in.astype(BF16)])
        kernel_sums = [[[jnp.zeros((8, LANES), F32)] * 4 for _ in range(3)] for _ in range(2)]
        for b in (1, 0):
            part = slice(b * BLK, (b + 1) * BLK)
            for h in range(2):
                c = slice(h * LANES, (h + 1) * LANES)
                q, k, v, g = (store[i, m, part, c] for m in range(4))
                row = table[h : h + 1, part]

                def weight(s, t):
                    mine = jnp.exp2(
                        (row[:, t * HALF : (t + 1) * HALF] - 7.0)
                        - down(row[:, s * HALF : (s + 1) * HALF])
                    )
                    return jnp.where(causal, mine, 0.0) if s == t else mine

                top = jnp.concatenate([weight(0, 0), weight(0, 1)], axis=1)
                low = weight(1, 1)

                def masked(full):
                    upper = (full[:HALF] * top).astype(BF16)
                    lower = (full[HALF:, HALF:] * low).astype(BF16)
                    return jnp.concatenate(
                        [upper, jnp.concatenate([blank, lower], axis=1)], axis=0
                    )

                gt = masked(dot(v, g, NT))
                pt = masked(dot(k, q, NT))
                wg, wk, wv = (scaled[m, i, part, c] for m in range(3))
                before, after = incoming[h][b], future[h][b]
                grads = (
                    dot(gt, k, TN) + dot(wg, before, NT),
                    dot(gt, q, NN) + dot(wv, after, NT),
                    dot(pt, g, NN) + dot(wk, after, NN),
                )
                for m in range(3):
                    for half in (1, 0):
                        at = RIM + b * BLK + half * HALF
                        mine = grads[m][half * HALF : (half + 1) * HALF]
                        for j in range(4):
                            product = xs[i, h, m, at - j : at - j + HALF] * mine
                            kernel_sums[h][m][j] = kernel_sums[h][m][j] + jnp.sum(
                                product.reshape(HALF // 8, 8, LANES), axis=0
                            )
                        xs[i, h, m, at : at + HALF] = mine
        for h in range(2):
            sums = [
                jnp.sum(kernel_sums[h][m][j], axis=0, keepdims=True)
                for m in range(3)
                for j in range(4)
            ]
            terms[:, columns(i, h, LANES)] = jnp.concatenate(
                sums + [jnp.zeros((4, LANES), F32)], axis=0
            )
        if remote:
            rim_copy(i).start()
        span = 3 * PAIR
        start = (i // 3) * (span // share)
        for r, (low_piece, high_piece) in enumerate(PIECES):

            @pl.when(lax.rem(i, 3) == r)
            def _():
                block = terms[:, pl.ds(pl.multiple_of((i // 3) * span, LANES), span)]
                for p in range(low_piece, high_piece):
                    piece = block[:, p * share : (p + 1) * share]
                    wide = jnp.concatenate([piece, jnp.zeros((16, 64 - share), F32)], axis=1)
                    pieces[start + p] = jnp.concatenate([wide[:8], wide[8:]], axis=1)
                if remote:

                    @functools.partial(loop, high_piece - low_piece)
                    def _(p):
                        owner = start + low_piece + p

                        @pl.when(owner != dp)
                        def _():
                            slot = lax.rem(dp - owner + peers, peers)
                            remote_copy(
                                pieces.at[owner], landed.at[slot], piece_send, piece_recv,
                                {"dp": owner},
                            ).start()

    @functools.partial(loop, steps)
    def _(i):
        if remote:
            rim_copy(i).wait()
        for m in range(3):
            for h in range(2):
                c = slice(h * LANES, (h + 1) * LANES)
                tail = slice(RIM + length, RIM + length + 8)
                xs[i, h, m, tail] = jnp.where(core == 0, xs[i, h, m, tail], 0.0)
                taps = [w_ref[m, j : j + 1, columns(i, h, LANES)] for j in range(4)]
                for r in range(0, length, CHUNK):
                    at = RIM + r
                    acc = taps[0] * xs[i, h, m, at : at + CHUNK]
                    for j in range(1, 4):
                        acc = acc + taps[j] * xs[i, h, m, at + j : at + j + CHUNK]
                    store[i, m, r : r + CHUNK, c] = acc.astype(BF16)
        for m in range(3):
            flush(i, m).start()

    if remote:
        others = pl.ds(1, peers - 1)
        remote_copy(pieces.at[others], landed.at[others], piece_send, piece_recv, other).wait()
        total = pieces[dp] + jnp.sum(landed[1:], axis=0)
        part_out[...] = total
        copy = remote_copy(part_out, part_in, part_send, part_recv, other)
        copy.start()
        copy.wait()
        total = (total + part_in[...]) * (1.0 / peers)
    else:
        total = pieces[dp]
    kernel_grad_ref[0] = total[0:4, :share]
    kernel_grad_ref[1] = total[4:8, :share]
    kernel_grad_ref[2] = total[0:4, 64 : 64 + share]

    @functools.partial(loop, steps)
    def _(i):
        for m in range(3):
            flush(i, m).wait()


def gradients(query, key, value, out_grad, log_decay, conv_kernel, remote=True):
    _, length, width = query.shape
    heads = log_decay.shape[1]
    steps = width // PAIR
    peers = lax.axis_size("dp") if remote else 64
    dma = pltpu.SemaphoreType.DMA
    anywhere = pl.BlockSpec(memory_space=pl.ANY)
    vmem = pl.BlockSpec(memory_space=pltpu.VMEM)
    halo = rims(query, key, value) if remote else jnp.zeros((3, RIM, width), BF16)
    return pl.pallas_call(
        functools.partial(main_kernel, remote),
        in_specs=[anywhere] * 4 + [vmem] * 3,
        out_specs=[anywhere] * 3 + [vmem],
        out_shape=[jax.ShapeDtypeStruct((1, length, width), BF16)] * 3
        + [jax.ShapeDtypeStruct((3, 4, width // peers), F32)],
        scratch_shapes=[
            pltpu.VMEM((steps, 2, 3, RIM + length + 8, LANES), F32),
            pltpu.VMEM((steps, 4, length, PAIR), BF16),
            pltpu.VMEM((3, steps, length, PAIR), BF16),
            pltpu.VMEM((steps, 8, length), F32),
            pltpu.VMEM((heads, LANES, LANES), F32),
            pltpu.VMEM((heads, LANES, LANES), F32),
            pltpu.VMEM((heads, LANES, LANES), BF16),
            pltpu.VMEM((heads, LANES, LANES), BF16),
            pltpu.VMEM((16, width), F32),
            pltpu.VMEM((peers, 8, LANES), F32),
            pltpu.VMEM((peers, 8, LANES), F32),
            pltpu.VMEM((8, LANES), F32),
            pltpu.VMEM((8, LANES), F32),
            dma((steps, 4)), dma((steps, 3)),
            dma((steps,)), dma((steps,)), dma((steps,)), dma((steps,)),
            dma, dma, dma, dma,
        ],
        compiler_params=pltpu.CompilerParams(
            collective_id=1 if remote else None,
            has_side_effects=True,
            vmem_limit_bytes=60 * 1024 * 1024,
        ),
        name="gradients",
    )(query, key, value, out_grad, halo, log_decay[0], conv_kernel)


def local(query, key, value, out_grad, log_decay, conv_kernel):
    return tuple(gradients(query, key, value, out_grad, log_decay, conv_kernel))


def solution(mesh):
    rows = P("dp", "ctx", None)
    return jax.shard_map(
        local,
        mesh=mesh,
        in_specs=(rows, rows, rows, rows, P("dp", None, "ctx"), P()),
        out_specs=(rows, rows, rows, P(None, None, "dp")),
        check_vma=False,
    )
```

```python
import functools

import jax
import jax.numpy as jnp
from jax import lax
from jax.experimental import pallas as pl
from jax.experimental.pallas import tpu as pltpu
from jax.sharding import PartitionSpec as P

MESH = pl.DeviceIdType.MESH
BLK = 256
HALF = 128
LANES = 128
PAIR = 256
RIM = 16
CHUNK = 64
PIECES = ((0, 5), (5, 10), (10, 16))
LOG2E = 1.4426950408889634
F32 = jnp.float32
BF16 = jnp.bfloat16
NT = (((1,), (1,)), ((), ()))
TN = (((0,), (0,)), ((), ()))
NN = (((1,), (0,)), ((), ()))


def dot(a, b, dims):
    return lax.dot_general(a, b, dims, preferred_element_type=F32)


def decay_tables(ld_ref, rows):
    upper = (
        lax.broadcasted_iota(jnp.int32, (BLK, BLK), 0)
        <= lax.broadcasted_iota(jnp.int32, (BLK, BLK), 1)
    ).astype(F32)
    heads, length = ld_ref.shape
    for b in range(length // BLK):
        span = slice(b * BLK, (b + 1) * BLK)
        sums = LOG2E * jnp.dot(
            ld_ref[:, span], upper, precision=lax.Precision.HIGHEST, preferred_element_type=F32
        )
        grown = jnp.exp2(sums)
        left = jnp.exp2(sums[:, BLK - 1 : BLK] - sums)
        for i in range(heads // 2):
            pair = slice(2 * i, 2 * i + 2)
            rows[i, :, span] = jnp.concatenate(
                [sums[pair], grown[pair], left[pair], jnp.zeros((2, BLK), F32)], axis=0
            )


def down(row):
    return jnp.broadcast_to(row, (LANES, LANES)).T


def diagonal(a, b):
    zero = jnp.zeros_like(a)
    return jnp.concatenate(
        [jnp.concatenate([a, zero], axis=1), jnp.concatenate([zero, b], axis=1)], axis=0
    )


def rim_kernel(q_any, k_any, v_any, halo_any, send_sem, recv_sem):
    length = q_any.shape[1]
    other = {"ctx": 1 - lax.axis_index("ctx")}
    barrier = pltpu.get_barrier_semaphore()
    pl.semaphore_signal(barrier, inc=1, device_id=other, device_id_type=MESH)
    pl.semaphore_wait(barrier, 1)
    copies = [
        pltpu.make_async_remote_copy(
            src_ref=source.at[0, pl.ds(length - RIM, RIM), :],
            dst_ref=halo_any.at[m],
            send_sem=send_sem.at[m],
            recv_sem=recv_sem.at[m],
            device_id=other,
            device_id_type=MESH,
        )
        for m, source in enumerate((q_any, k_any, v_any))
    ]
    for copy in copies:
        copy.start()
    for copy in copies:
        copy.wait()


def rims(query, key, value):
    return pl.pallas_call(
        rim_kernel,
        in_specs=[pl.BlockSpec(memory_space=pl.ANY)] * 3,
        out_specs=pl.BlockSpec(memory_space=pltpu.VMEM),
        out_shape=pltpu.VMEM((3, RIM, query.shape[2]), BF16),
        scratch_shapes=[pltpu.SemaphoreType.DMA((3,)), pltpu.SemaphoreType.DMA((3,))],
        compiler_params=pltpu.CompilerParams(collective_id=0, has_side_effects=True),
        name="rims",
    )(*(pltpu.with_memory_space_constraint(x, pltpu.HBM) for x in (query, key, value)))


def main_kernel(
    remote,
    q_any, k_any, v_any, g_any, halo_ref, ld_ref, w_ref,
    store, kernel_grad_ref,
    xs, scaled, rows, s_first, f_last, msg_out, msg_in,
    terms, pieces, landed, part_out, part_in,
    in_sem, msg_send, msg_recv, rim_send, rim_recv, piece_send, piece_recv, part_send,
    part_recv,
):
    steps, _, length, _ = store.shape
    core = lax.axis_index("ctx") if remote else 0
    dp = lax.axis_index("dp") if remote else 0
    peers = pieces.shape[0]
    other = {"ctx": 1 - core}
    share = terms.shape[1] // peers

    def columns(i, h=0, width=PAIR):
        return pl.ds(pl.multiple_of(i * PAIR + h * LANES, LANES), width)

    def fetch(i, m):
        source = (q_any, k_any, v_any, g_any)[m]
        return pltpu.make_async_copy(source.at[0, :, columns(i)], store.at[i, m], in_sem.at[i, m])

    def remote_copy(source, target, send_sem, recv_sem, device):
        return pltpu.make_async_remote_copy(
            src_ref=source, dst_ref=target, send_sem=send_sem, recv_sem=recv_sem,
            device_id=device, device_id_type=MESH,
        )

    def state_copy(i):
        pair = pl.ds(2 * i, 2)
        return remote_copy(msg_out.at[pair], msg_in.at[pair], msg_send.at[i], msg_recv.at[i], other)

    def rim_copy(i):
        return remote_copy(
            xs.at[i, :, :, pl.ds(RIM, 8), :], xs.at[i, :, :, pl.ds(RIM + length, 8), :],
            rim_send.at[i], rim_recv.at[i], other,
        )

    def loop(count, body):
        def step(i, carry):
            body(i)
            return carry

        lax.fori_loop(0, count, step, 0)

    @functools.partial(loop, steps)
    def _(i):
        for m in range(4):
            fetch(i, m).start()

    if remote:
        barrier = pltpu.get_barrier_semaphore()
        pl.semaphore_signal(barrier, inc=1, device_id=other, device_id_type=MESH)

        @functools.partial(loop, peers - 1)
        def _(d):
            peer = {"dp": lax.rem(dp + d + 1, peers)}
            pl.semaphore_signal(barrier, inc=1, device_id=peer, device_id_type=MESH)
    else:
        msg_in[...] = jnp.zeros_like(msg_in)

    decay_tables(ld_ref, rows)
    first, last = pl.ds(0, BLK), pl.ds(BLK, BLK)
    own = pl.ds(pl.multiple_of((1 - core) * BLK, BLK), BLK)

    def states(i):
        table = rows[i]
        state = dot(store[i, 1, first, :], scaled[2, i, first, :], TN)
        future = dot(store[i, 0, last, :], scaled[0, i, last, :], TN)
        message = dot(store[i, 1 - core, own, :], scaled[2 - 2 * core, i, own, :], TN)
        for h in range(2):
            c = slice(h * LANES, (h + 1) * LANES)
            decay = [table[2 + h : 3 + h, (b + 1) * BLK - 1 : (b + 1) * BLK] for b in range(2)]
            s_first[2 * i + h] = state[c, c]
            f_last[2 * i + h] = future[c, c]
            msg_out[2 * i + h] = (
                message[c, c]
                + jnp.where(core == 0, decay[1] * state[c, c], decay[0] * future[c, c])
            ).astype(BF16)

    def spread(i, h, low, high):
        c = slice(h * LANES, (h + 1) * LANES)
        for m in range(3):
            taps = [w_ref[m, j : j + 1, columns(i, h, LANES)] for j in range(4)]
            for r in range(low, high, CHUNK):
                size = min(CHUNK, high - r)
                at = RIM + r
                acc = taps[0] * xs[i, h, m, at : at + size]
                for j in range(1, 4):
                    acc = acc + taps[j] * xs[i, h, m, at + j : at + j + size]
                store[i, m, r : r + size, c] = acc.astype(BF16)

    @functools.partial(loop, steps)
    def _(i):
        for m in range(4):
            fetch(i, m).wait()
        if remote:

            @pl.when(i == steps - 1)
            def _():
                pl.semaphore_wait(pltpu.get_barrier_semaphore(), peers)
                loop(steps - 2, lambda n: state_copy(n).start())

        states(jnp.maximum(i - 1, 0))
        table = rows[i]
        for h in range(2):
            c = slice(h * LANES, (h + 1) * LANES)
            for m in range(3):
                before = halo_ref[m, :, columns(i, h, LANES)].astype(F32)
                xs[i, h, m, 0:RIM] = jnp.where(core == 1, before, 0.0)
                for r in range(0, length, CHUNK):
                    xs[i, h, m, RIM + r : RIM + r + CHUNK] = store[i, m, r : r + CHUNK, c].astype(F32)
            taps = [[w_ref[m, j : j + 1, columns(i, h, LANES)] for j in range(4)] for m in range(3)]
            for base in range(0, length, LANES):
                grown = down(table[2 + h : 3 + h, base : base + LANES])
                left = down(table[4 + h : 5 + h, base : base + LANES])
                for r in range(0, LANES, CHUNK):
                    part = slice(base + r, base + r + CHUNK)
                    near = slice(r, r + CHUNK)
                    for m in range(3):
                        at = RIM + base + r
                        acc = taps[m][0] * xs[i, h, m, at : at + CHUNK]
                        for j in range(1, 4):
                            acc = acc + taps[m][j] * xs[i, h, m, at - j : at - j + CHUNK]
                        store[i, m, part, c] = acc.astype(BF16)
                        if m > 0:
                            scaled[m, i, part, c] = (acc * left[near]).astype(BF16)
                    scaled[0, i, part, c] = (store[i, 3, part, c].astype(F32) * grown[near]).astype(BF16)

    states(steps - 1)
    if remote:
        state_copy(steps - 2).start()
        state_copy(steps - 1).start()

    @functools.partial(loop, steps)
    def _(i):
        if remote:
            state_copy(i).wait()
        table = rows[i]
        scale = 1.0 / LANES
        causal = lax.broadcasted_iota(jnp.int32, (HALF, HALF), 0) <= lax.broadcasted_iota(
            jnp.int32, (HALF, HALF), 1
        )
        blank = jnp.zeros((HALF, HALF), BF16)
        incoming, future = [], []
        for h in range(2):
            decay = [table[2 + h : 3 + h, (b + 1) * BLK - 1 : (b + 1) * BLK] for b in range(2)]
            message = msg_in[2 * i + h].astype(F32) * scale
            state_in = jnp.where(core == 1, message, 0.0)
            future_in = jnp.where(core == 0, message, 0.0)
            state = decay[0] * state_in + scale * s_first[2 * i + h]
            grads = decay[1] * future_in + scale * f_last[2 * i + h]
            incoming.append([state_in.astype(BF16), state.astype(BF16)])
            future.append([grads.astype(BF16), future_in.astype(BF16)])
        kernel_sums = [[[jnp.zeros((8, LANES), F32)] * 4 for _ in range(3)] for _ in range(2)]
        for h in range(2):
            c = slice(h * LANES, (h + 1) * LANES)
            for b in (1, 0):
                part = slice(b * BLK, (b + 1) * BLK)
                q, k, v, g = (store[i, m, part, c] for m in range(4))
                row = table[h : h + 1, part]

                def weight(s, t):
                    mine = jnp.exp2(
                        (row[:, t * HALF : (t + 1) * HALF] - 7.0)
                        - down(row[:, s * HALF : (s + 1) * HALF])
                    )
                    return jnp.where(causal, mine, 0.0) if s == t else mine

                top = jnp.concatenate([weight(0, 0), weight(0, 1)], axis=1)
                low = weight(1, 1)

                def masked(full):
                    upper = (full[:HALF] * top).astype(BF16)
                    lower = (full[HALF:, HALF:] * low).astype(BF16)
                    return jnp.concatenate(
                        [upper, jnp.concatenate([blank, lower], axis=1)], axis=0
                    )

                gt = masked(dot(v, g, NT))
                pt = masked(dot(k, q, NT))
                wg, wk, wv = (scaled[m, i, part, c] for m in range(3))
                before, after = incoming[h][b], future[h][b]
                grads = (
                    dot(gt, k, TN) + dot(wg, before, NT),
                    dot(gt, q, NN) + dot(wv, after, NT),
                    dot(pt, g, NN) + dot(wk, after, NN),
                )
                for m in range(3):
                    for half in (1, 0):
                        at = RIM + b * BLK + half * HALF
                        mine = grads[m][half * HALF : (half + 1) * HALF]
                        for j in range(4):
                            product = xs[i, h, m, at - j : at - j + HALF] * mine
                            kernel_sums[h][m][j] = kernel_sums[h][m][j] + jnp.sum(
                                product.reshape(HALF // 8, 8, LANES), axis=0
                            )
                        xs[i, h, m, at : at + HALF] = mine
            if h == 0:
                spread(i, h, 0, length - RIM)
        for h in range(2):
            sums = [
                jnp.sum(kernel_sums[h][m][j], axis=0, keepdims=True)
                for m in range(3)
                for j in range(4)
            ]
            terms[:, columns(i, h, LANES)] = jnp.concatenate(
                sums + [jnp.zeros((4, LANES), F32)], axis=0
            )
        if remote:
            rim_copy(i).start()
        span = 3 * PAIR
        start = (i // 3) * (span // share)
        for r, (low_piece, high_piece) in enumerate(PIECES):

            @pl.when(lax.rem(i, 3) == r)
            def _():
                block = terms[:, pl.ds(pl.multiple_of((i // 3) * span, LANES), span)]
                for p in range(low_piece, high_piece):
                    piece = block[:, p * share : (p + 1) * share]
                    wide = jnp.concatenate([piece, jnp.zeros((16, 64 - share), F32)], axis=1)
                    pieces[start + p] = jnp.concatenate([wide[:8], wide[8:]], axis=1)
                if remote:

                    @functools.partial(loop, high_piece - low_piece)
                    def _(p):
                        owner = start + low_piece + p

                        @pl.when(owner != dp)
                        def _():
                            slot = lax.rem(dp - owner + peers, peers)
                            remote_copy(
                                pieces.at[owner], landed.at[slot], piece_send, piece_recv,
                                {"dp": owner},
                            ).start()

    @functools.partial(loop, steps)
    def _(i):
        if remote:
            rim_copy(i).wait()
        tail = slice(RIM + length, RIM + length + 8)
        for h in range(2):
            for m in range(3):
                xs[i, h, m, tail] = jnp.where(core == 0, xs[i, h, m, tail], 0.0)
        spread(i, 0, length - RIM, length)
        spread(i, 1, 0, length)

    if remote:
        others = pl.ds(1, peers - 1)
        remote_copy(pieces.at[others], landed.at[others], piece_send, piece_recv, other).wait()
        total = pieces[dp] + jnp.sum(landed[1:], axis=0)
        part_out[...] = total
        copy = remote_copy(part_out, part_in, part_send, part_recv, other)
        copy.start()
        copy.wait()
        total = (total + part_in[...]) * (1.0 / peers)
    else:
        total = pieces[dp]
    kernel_grad_ref[0] = total[0:4, :share]
    kernel_grad_ref[1] = total[4:8, :share]
    kernel_grad_ref[2] = total[0:4, 64 : 64 + share]


def gradients(query, key, value, out_grad, log_decay, conv_kernel, remote=True):
    _, length, width = query.shape
    heads = log_decay.shape[1]
    steps = width // PAIR
    peers = lax.axis_size("dp") if remote else 64
    dma = pltpu.SemaphoreType.DMA
    anywhere = pl.BlockSpec(memory_space=pl.ANY)
    vmem = pl.BlockSpec(memory_space=pltpu.VMEM)
    if remote:
        halo = pltpu.with_memory_space_constraint(rims(query, key, value), pltpu.VMEM)
    else:
        halo = jnp.zeros((3, RIM, width), BF16)
    return pl.pallas_call(
        functools.partial(main_kernel, remote),
        in_specs=[anywhere] * 4 + [vmem] * 3,
        out_specs=[vmem, vmem],
        out_shape=[
            pltpu.VMEM((steps, 4, length, PAIR), BF16),
            pltpu.VMEM((3, 4, width // peers), F32),
        ],
        scratch_shapes=[
            pltpu.VMEM((steps, 2, 3, RIM + length + 8, LANES), F32),
            pltpu.VMEM((3, steps, length, PAIR), BF16),
            pltpu.VMEM((steps, 8, length), F32),
            pltpu.VMEM((heads, LANES, LANES), F32),
            pltpu.VMEM((heads, LANES, LANES), F32),
            pltpu.VMEM((heads, LANES, LANES), BF16),
            pltpu.VMEM((heads, LANES, LANES), BF16),
            pltpu.VMEM((16, width), F32),
            pltpu.VMEM((peers, 8, LANES), F32),
            pltpu.VMEM((peers, 8, LANES), F32),
            pltpu.VMEM((8, LANES), F32),
            pltpu.VMEM((8, LANES), F32),
            dma((steps, 4)),
            dma((steps,)), dma((steps,)), dma((steps,)), dma((steps,)),
            dma, dma, dma, dma,
        ],
        compiler_params=pltpu.CompilerParams(
            collective_id=1 if remote else None,
            has_side_effects=True,
            vmem_limit_bytes=46 * 1024 * 1024,
        ),
        name="gradients",
    )(query, key, value, out_grad, halo, log_decay[0], conv_kernel)


def flush_kernel(store, kernel_grad_in, oq_any, ok_any, ov_any, kernel_grad_out, sem):
    steps = store.shape[0]
    copies = [
        pltpu.make_async_copy(
            store.at[i, m], out.at[0, :, pl.ds(i * PAIR, PAIR)], sem.at[i, m]
        )
        for i in range(steps)
        for m, out in enumerate((oq_any, ok_any, ov_any))
    ]
    for copy in copies:
        copy.start()
    kernel_grad_out[...] = kernel_grad_in[...]
    for copy in copies:
        copy.wait()


def flush(store, kernel_grad):
    steps, _, length, _ = store.shape
    anywhere = pl.BlockSpec(memory_space=pl.ANY)
    vmem = pl.BlockSpec(memory_space=pltpu.VMEM)
    return pl.pallas_call(
        flush_kernel,
        in_specs=[anywhere, vmem],
        out_specs=[anywhere] * 3 + [vmem],
        out_shape=[jax.ShapeDtypeStruct((1, length, steps * PAIR), BF16)] * 3
        + [jax.ShapeDtypeStruct(kernel_grad.shape, F32)],
        scratch_shapes=[pltpu.SemaphoreType.DMA((steps, 3))],
        compiler_params=pltpu.CompilerParams(vmem_limit_bytes=16 * 1024 * 1024),
        name="flush",
    )(*(pltpu.with_memory_space_constraint(x, pltpu.VMEM) for x in (store, kernel_grad)))


def local(query, key, value, out_grad, log_decay, conv_kernel):
    store, kernel_grad = gradients(query, key, value, out_grad, log_decay, conv_kernel)
    return tuple(flush(store, kernel_grad))


def solution(mesh):
    rows = P("dp", "ctx", None)
    return jax.shard_map(
        local,
        mesh=mesh,
        in_specs=(rows, rows, rows, rows, P("dp", None, "ctx"), P()),
        out_specs=(rows, rows, rows, P(None, None, "dp")),
        check_vma=False,
    )
```

```python
import functools

import jax
import jax.numpy as jnp
from jax import lax
from jax.experimental import pallas as pl
from jax.experimental.pallas import tpu as pltpu
from jax.sharding import PartitionSpec as P

MESH = pl.DeviceIdType.MESH
BLK = 256
HALF = 128
LANES = 128
PAIR = 256
RIM = 16
CHUNK = 64
PIECES = ((0, 5), (5, 10), (10, 16))
LOG2E = 1.4426950408889634
F32 = jnp.float32
BF16 = jnp.bfloat16
NT = (((1,), (1,)), ((), ()))
TN = (((0,), (0,)), ((), ()))
NN = (((1,), (0,)), ((), ()))


def dot(a, b, dims):
    return lax.dot_general(a, b, dims, preferred_element_type=F32)


def decay_tables(ld_ref, rows):
    upper = (
        lax.broadcasted_iota(jnp.int32, (BLK, BLK), 0)
        <= lax.broadcasted_iota(jnp.int32, (BLK, BLK), 1)
    ).astype(F32)
    heads, length = ld_ref.shape
    for b in range(length // BLK):
        span = slice(b * BLK, (b + 1) * BLK)
        sums = LOG2E * jnp.dot(
            ld_ref[:, span], upper, precision=lax.Precision.HIGHEST, preferred_element_type=F32
        )
        grown = jnp.exp2(sums)
        left = jnp.exp2(sums[:, BLK - 1 : BLK] - sums)
        for i in range(heads // 2):
            pair = slice(2 * i, 2 * i + 2)
            rows[i, :, span] = jnp.concatenate(
                [sums[pair], grown[pair], left[pair], sums[pair] - 7.0], axis=0
            )


def down(row):
    return jnp.broadcast_to(row, (LANES, LANES)).T


def diagonal(a, b):
    zero = jnp.zeros_like(a)
    return jnp.concatenate(
        [jnp.concatenate([a, zero], axis=1), jnp.concatenate([zero, b], axis=1)], axis=0
    )


def prepare_kernel(
    remote, q_any, k_any, v_any, ld_any, w_any, halo, rows, taps, ld, send_sem, recv_sem, local_sem
):
    length = q_any.shape[1]
    local = [
        pltpu.make_async_copy(ld_any, ld, local_sem.at[0]),
        pltpu.make_async_copy(w_any, taps, local_sem.at[1]),
    ]
    for copy in local:
        copy.start()
    copies = []
    if remote:
        other = {"ctx": 1 - lax.axis_index("ctx")}
        barrier = pltpu.get_barrier_semaphore()
        pl.semaphore_signal(barrier, inc=1, device_id=other, device_id_type=MESH)
        pl.semaphore_wait(barrier, 1)
        copies = [
            pltpu.make_async_remote_copy(
                src_ref=source.at[0, pl.ds(length - RIM, RIM), :],
                dst_ref=halo.at[m],
                send_sem=send_sem.at[m],
                recv_sem=recv_sem.at[m],
                device_id=other,
                device_id_type=MESH,
            )
            for m, source in enumerate((q_any, k_any, v_any))
        ]
    else:
        halo[...] = jnp.zeros_like(halo)
    for copy in copies:
        copy.start()
    local[0].wait()
    decay_tables(ld, rows)
    local[1].wait()
    for copy in copies:
        copy.wait()


def prepare(query, key, value, log_decay, conv_kernel, remote):
    _, length, width = query.shape
    heads = log_decay.shape[0]
    anywhere = pl.BlockSpec(memory_space=pl.ANY)
    vmem = pl.BlockSpec(memory_space=pltpu.VMEM)
    dma = pltpu.SemaphoreType.DMA
    inputs = (query, key, value, log_decay, conv_kernel)
    return pl.pallas_call(
        functools.partial(prepare_kernel, remote),
        in_specs=[anywhere] * 5,
        out_specs=[vmem] * 3,
        out_shape=[
            pltpu.VMEM((3, RIM, width), BF16),
            pltpu.VMEM((heads // 2, 8, length), F32),
            pltpu.VMEM(conv_kernel.shape, F32),
        ],
        scratch_shapes=[pltpu.VMEM((heads, length), F32), dma((3,)), dma((3,)), dma((2,))],
        compiler_params=pltpu.CompilerParams(
            collective_id=0 if remote else None, has_side_effects=True
        ),
        name="prepare",
    )(*(pltpu.with_memory_space_constraint(x, pltpu.HBM) for x in inputs))


def main_kernel(
    remote,
    q_any, k_any, v_any, g_any, halo_ref, rows, w_ref,
    store, kernel_grad_ref,
    xs, scaled, s_first, f_last, msg_out, msg_in, rim_out, rim_in,
    terms, pieces, landed, part_out, part_in,
    in_sem, msg_send, msg_recv, rim_send, rim_recv, piece_send, piece_recv, part_send,
    part_recv,
):
    steps, _, length, _ = store.shape
    core = lax.axis_index("ctx") if remote else 0
    dp = lax.axis_index("dp") if remote else 0
    peers = pieces.shape[0]
    other = {"ctx": 1 - core}
    share = terms.shape[1] // peers

    def columns(i, h=0, width=PAIR):
        return pl.ds(pl.multiple_of(i * PAIR + h * LANES, LANES), width)

    def fetch(i, m):
        source = (q_any, k_any, v_any, g_any)[m]
        return pltpu.make_async_copy(source.at[0, :, columns(i)], store.at[i, m], in_sem.at[i, m])

    def remote_copy(source, target, send_sem, recv_sem, device):
        return pltpu.make_async_remote_copy(
            src_ref=source, dst_ref=target, send_sem=send_sem, recv_sem=recv_sem,
            device_id=device, device_id_type=MESH,
        )

    state_spans = ((0, 2), (2, steps - 2), (steps - 2, steps))
    rim_spans = ((0, steps // 2), (steps // 2, steps))

    def state_copy(n):
        low, high = state_spans[n]
        span = pl.ds(2 * low, 2 * (high - low))
        return remote_copy(msg_out.at[span], msg_in.at[span], msg_send.at[n], msg_recv.at[n], other)

    def rim_copy(n):
        low, high = rim_spans[n]
        span = pl.ds(low, high - low)
        return remote_copy(rim_out.at[span], rim_in.at[span], rim_send.at[n], rim_recv.at[n], other)

    def loop(count, body):
        def step(i, carry):
            body(i)
            return carry

        lax.fori_loop(0, count, step, 0)

    @functools.partial(loop, steps)
    def _(i):
        for m in range(4):
            fetch(i, m).start()

    if remote:
        barrier = pltpu.get_barrier_semaphore()
        pl.semaphore_signal(barrier, inc=1, device_id=other, device_id_type=MESH)

        @functools.partial(loop, peers - 1)
        def _(d):
            peer = {"dp": lax.rem(dp + d + 1, peers)}
            pl.semaphore_signal(barrier, inc=1, device_id=peer, device_id_type=MESH)
    else:
        msg_in[...] = jnp.zeros_like(msg_in)

    first, last = pl.ds(0, BLK), pl.ds(BLK, BLK)

    def states(i):
        table = rows[i]
        state = dot(store[i, 1, first, :], scaled[2, i, first, :], TN)
        future = dot(store[i, 0, last, :], scaled[0, i, last, :], TN)
        message = dot(
            jnp.where(core == 0, store[i, 1, last, :], store[i, 0, first, :]),
            jnp.where(core == 0, scaled[2, i, last, :], scaled[0, i, first, :]),
            TN,
        )
        for h in range(2):
            c = slice(h * LANES, (h + 1) * LANES)
            decay = [table[2 + h : 3 + h, (b + 1) * BLK - 1 : (b + 1) * BLK] for b in range(2)]
            s_first[2 * i + h] = state[c, c]
            f_last[2 * i + h] = future[c, c]
            msg_out[2 * i + h] = (
                message[c, c]
                + jnp.where(core == 0, decay[1] * state[c, c], decay[0] * future[c, c])
            ).astype(BF16)

    def spread(i, h, low, high):
        c = slice(h * LANES, (h + 1) * LANES)
        for m in range(3):
            taps = [w_ref[m, j : j + 1, columns(i, h, LANES)] for j in range(4)]
            for r in range(low, high, CHUNK):
                size = min(CHUNK, high - r)
                at = RIM + r
                acc = taps[0] * xs[i, h, m, at : at + size]
                for j in range(1, 4):
                    acc = acc + taps[j] * xs[i, h, m, at + j : at + j + size]
                store[i, m, r : r + size, c] = acc.astype(BF16)

    @functools.partial(loop, steps)
    def _(i):
        for m in range(4):
            fetch(i, m).wait()
        if remote:

            @pl.when(i == steps - 1)
            def _():
                pl.semaphore_wait(pltpu.get_barrier_semaphore(), peers)
                state_copy(0).start()
                state_copy(1).start()

        states(jnp.maximum(i - 1, 0))
        table = rows[i]
        for h in range(2):
            c = slice(h * LANES, (h + 1) * LANES)
            for m in range(3):
                before = halo_ref[m, :, columns(i, h, LANES)].astype(F32)
                xs[i, h, m, 0:RIM] = jnp.where(core == 1, before, 0.0)
                for r in range(0, length, CHUNK):
                    xs[i, h, m, RIM + r : RIM + r + CHUNK] = store[i, m, r : r + CHUNK, c].astype(F32)
            taps = [[w_ref[m, j : j + 1, columns(i, h, LANES)] for j in range(4)] for m in range(3)]
            for base in range(0, length, LANES):
                grown = down(table[2 + h : 3 + h, base : base + LANES])
                left = down(table[4 + h : 5 + h, base : base + LANES])
                for r in range(0, LANES, CHUNK):
                    part = slice(base + r, base + r + CHUNK)
                    near = slice(r, r + CHUNK)
                    for m in range(3):
                        at = RIM + base + r
                        acc = taps[m][0] * xs[i, h, m, at : at + CHUNK]
                        for j in range(1, 4):
                            acc = acc + taps[m][j] * xs[i, h, m, at - j : at - j + CHUNK]
                        store[i, m, part, c] = acc.astype(BF16)
                        if m > 0:
                            scaled[m, i, part, c] = (acc * left[near]).astype(BF16)
                    scaled[0, i, part, c] = (store[i, 3, part, c].astype(F32) * grown[near]).astype(BF16)

    states(steps - 1)
    if remote:
        state_copy(2).start()

    @functools.partial(loop, steps)
    def _(i):
        if remote:
            for n, (low, _) in enumerate(state_spans):

                @pl.when(i == low)
                def _():
                    state_copy(n).wait()

        table = rows[i]
        scale = 1.0 / LANES
        causal = lax.broadcasted_iota(jnp.int32, (HALF, HALF), 0) <= lax.broadcasted_iota(
            jnp.int32, (HALF, HALF), 1
        )
        blank = jnp.zeros((HALF, HALF), BF16)
        incoming, future = [], []
        for h in range(2):
            decay = [table[2 + h : 3 + h, (b + 1) * BLK - 1 : (b + 1) * BLK] for b in range(2)]
            message = msg_in[2 * i + h].astype(F32) * scale
            state_in = jnp.where(core == 1, message, 0.0)
            future_in = jnp.where(core == 0, message, 0.0)
            state = decay[0] * state_in + scale * s_first[2 * i + h]
            grads = decay[1] * future_in + scale * f_last[2 * i + h]
            incoming.append([state_in.astype(BF16), state.astype(BF16)])
            future.append([grads.astype(BF16), future_in.astype(BF16)])
        kernel_sums = [[[jnp.zeros((8, LANES), F32)] * 4 for _ in range(3)] for _ in range(2)]
        for h in range(2):
            c = slice(h * LANES, (h + 1) * LANES)
            for b in (1, 0):
                part = slice(b * BLK, (b + 1) * BLK)
                q, k, v, g = (store[i, m, part, c] for m in range(4))
                row = table[h : h + 1, part]
                lowered = table[6 + h : 7 + h, part]

                def weight(s, t):
                    mine = jnp.exp2(
                        lowered[:, t * HALF : (t + 1) * HALF]
                        - down(row[:, s * HALF : (s + 1) * HALF])
                    )
                    return jnp.where(causal, mine, 0.0) if s == t else mine

                top = jnp.concatenate([weight(0, 0), weight(0, 1)], axis=1)
                low = weight(1, 1)

                def masked(full):
                    upper = (full[:HALF] * top).astype(BF16)
                    lower = (full[HALF:, HALF:] * low).astype(BF16)
                    return jnp.concatenate(
                        [upper, jnp.concatenate([blank, lower], axis=1)], axis=0
                    )

                gt = masked(dot(v, g, NT))
                pt = masked(dot(k, q, NT))
                wg, wk, wv = (scaled[m, i, part, c] for m in range(3))
                before, after = incoming[h][b], future[h][b]
                grads = (
                    dot(gt, k, TN) + dot(wg, before, NT),
                    dot(gt, q, NN) + dot(wv, after, NT),
                    dot(pt, g, NN) + dot(wk, after, NN),
                )
                for m in range(3):
                    for half in (1, 0):
                        at = RIM + b * BLK + half * HALF
                        mine = grads[m][half * HALF : (half + 1) * HALF]
                        for j in range(4):
                            product = xs[i, h, m, at - j : at - j + HALF] * mine
                            kernel_sums[h][m][j] = kernel_sums[h][m][j] + jnp.sum(
                                product.reshape(HALF // 8, 8, LANES), axis=0
                            )
                        xs[i, h, m, at : at + HALF] = mine
        for h in range(2):
            sums = [
                jnp.sum(kernel_sums[h][m][j], axis=0, keepdims=True)
                for m in range(3)
                for j in range(4)
            ]
            terms[:, columns(i, h, LANES)] = jnp.concatenate(
                sums + [jnp.zeros((4, LANES), F32)], axis=0
            )
        for h in range(2):
            for m in range(3):
                rim_out[i, h, m] = xs[i, h, m, RIM : RIM + 8]
        if remote:
            for n, (_, high) in enumerate(rim_spans):

                @pl.when(i == high - 1)
                def _():
                    rim_copy(n).start()

        span = 3 * PAIR
        start = (i // 3) * (span // share)
        for r, (low_piece, high_piece) in enumerate(PIECES):

            @pl.when(lax.rem(i, 3) == r)
            def _():
                block = terms[:, pl.ds(pl.multiple_of((i // 3) * span, LANES), span)]
                for p in range(low_piece, high_piece):
                    piece = block[:, p * share : (p + 1) * share]
                    wide = jnp.concatenate([piece, jnp.zeros((16, 64 - share), F32)], axis=1)
                    pieces[start + p] = jnp.concatenate([wide[:8], wide[8:]], axis=1)
                if remote:

                    @functools.partial(loop, high_piece - low_piece)
                    def _(p):
                        owner = start + low_piece + p

                        @pl.when(owner != dp)
                        def _():
                            slot = lax.rem(dp - owner + peers, peers)
                            remote_copy(
                                pieces.at[owner], landed.at[slot], piece_send, piece_recv,
                                {"dp": owner},
                            ).start()

    @functools.partial(loop, steps)
    def _(i):
        spread(i, 0, 0, length - RIM)
        spread(i, 1, 0, length - RIM)

    if remote:
        for n in range(len(rim_spans)):
            rim_copy(n).wait()

    @functools.partial(loop, steps)
    def _(i):
        tail = slice(RIM + length, RIM + length + 8)
        for h in range(2):
            for m in range(3):
                xs[i, h, m, tail] = jnp.where(core == 0, rim_in[i, h, m], 0.0)
            spread(i, h, length - RIM, length)

    if remote:
        others = pl.ds(1, peers - 1)
        remote_copy(pieces.at[others], landed.at[others], piece_send, piece_recv, other).wait()
        total = pieces[dp] + jnp.sum(landed[1:], axis=0)
        part_out[...] = total
        copy = remote_copy(part_out, part_in, part_send, part_recv, other)
        copy.start()
        copy.wait()
        total = (total + part_in[...]) * (1.0 / peers)
    else:
        total = pieces[dp]
    kernel_grad_ref[0] = total[0:4, :share]
    kernel_grad_ref[1] = total[4:8, :share]
    kernel_grad_ref[2] = total[0:4, 64 : 64 + share]


def gradients(query, key, value, out_grad, log_decay, conv_kernel, remote=True):
    _, length, width = query.shape
    heads = log_decay.shape[1]
    steps = width // PAIR
    peers = lax.axis_size("dp") if remote else 64
    dma = pltpu.SemaphoreType.DMA
    anywhere = pl.BlockSpec(memory_space=pl.ANY)
    vmem = pl.BlockSpec(memory_space=pltpu.VMEM)
    prepared = prepare(query, key, value, log_decay[0], conv_kernel, remote)
    prepared = [pltpu.with_memory_space_constraint(x, pltpu.VMEM) for x in prepared]
    return pl.pallas_call(
        functools.partial(main_kernel, remote),
        in_specs=[anywhere] * 4 + [vmem] * 3,
        out_specs=[vmem, vmem],
        out_shape=[
            pltpu.VMEM((steps, 4, length, PAIR), BF16),
            pltpu.VMEM((3, 4, width // peers), F32),
        ],
        scratch_shapes=[
            pltpu.VMEM((steps, 2, 3, RIM + length + 8, LANES), F32),
            pltpu.VMEM((3, steps, length, PAIR), BF16),
            pltpu.VMEM((heads, LANES, LANES), F32),
            pltpu.VMEM((heads, LANES, LANES), F32),
            pltpu.VMEM((heads, LANES, LANES), BF16),
            pltpu.VMEM((heads, LANES, LANES), BF16),
            pltpu.VMEM((steps, 2, 3, 8, LANES), F32),
            pltpu.VMEM((steps, 2, 3, 8, LANES), F32),
            pltpu.VMEM((16, width), F32),
            pltpu.VMEM((peers, 8, LANES), F32),
            pltpu.VMEM((peers, 8, LANES), F32),
            pltpu.VMEM((8, LANES), F32),
            pltpu.VMEM((8, LANES), F32),
            dma((steps, 4)),
            dma((3,)), dma((3,)), dma((2,)), dma((2,)),
            dma, dma, dma, dma,
        ],
        compiler_params=pltpu.CompilerParams(
            collective_id=1 if remote else None,
            has_side_effects=True,
            vmem_limit_bytes=46 * 1024 * 1024,
        ),
        name="gradients",
    )(
        *(pltpu.with_memory_space_constraint(x, pltpu.HBM) for x in (query, key, value, out_grad)),
        *prepared,
    )


def flush_kernel(store, kernel_grad_in, oq_any, ok_any, ov_any, kernel_grad_out, sem):
    steps = store.shape[0]
    copies = [
        pltpu.make_async_copy(
            store.at[i, m], out.at[0, :, pl.ds(i * PAIR, PAIR)], sem.at[i, m]
        )
        for i in range(steps)
        for m, out in enumerate((oq_any, ok_any, ov_any))
    ]
    for copy in copies:
        copy.start()
    kernel_grad_out[...] = kernel_grad_in[...]
    for copy in copies:
        copy.wait()


def flush(store, kernel_grad):
    steps, _, length, _ = store.shape
    anywhere = pl.BlockSpec(memory_space=pl.ANY)
    vmem = pl.BlockSpec(memory_space=pltpu.VMEM)
    return pl.pallas_call(
        flush_kernel,
        in_specs=[anywhere, vmem],
        out_specs=[anywhere] * 3 + [vmem],
        out_shape=[jax.ShapeDtypeStruct((1, length, steps * PAIR), BF16)] * 3
        + [jax.ShapeDtypeStruct(kernel_grad.shape, F32)],
        scratch_shapes=[pltpu.SemaphoreType.DMA((steps, 3))],
        compiler_params=pltpu.CompilerParams(vmem_limit_bytes=16 * 1024 * 1024),
        name="flush",
    )(*(pltpu.with_memory_space_constraint(x, pltpu.VMEM) for x in (store, kernel_grad)))


def local(query, key, value, out_grad, log_decay, conv_kernel):
    store, kernel_grad = gradients(query, key, value, out_grad, log_decay, conv_kernel)
    return tuple(flush(store, kernel_grad))


def solution(mesh):
    rows = P("dp", "ctx", None)
    return jax.shard_map(
        local,
        mesh=mesh,
        in_specs=(rows, rows, rows, rows, P("dp", None, "ctx"), P()),
        out_specs=(rows, rows, rows, P(None, None, "dp")),
        check_vma=False,
    )
```

```python
import functools

import jax
import jax.numpy as jnp
from jax import lax
from jax.experimental import pallas as pl
from jax.experimental.pallas import tpu as pltpu
from jax.sharding import PartitionSpec as P

MESH = pl.DeviceIdType.MESH
BLK = 256
HALF = 128
LANES = 128
PAIR = 256
RIM = 16
CHUNK = 64
LOG2E = 1.4426950408889634
F32 = jnp.float32
BF16 = jnp.bfloat16
NT = (((1,), (1,)), ((), ()))
TN = (((0,), (0,)), ((), ()))
NN = (((1,), (0,)), ((), ()))


def dot(a, b, dims):
    return lax.dot_general(a, b, dims, preferred_element_type=F32)


def decay_tables(ld_ref, rows):
    upper = (
        lax.broadcasted_iota(jnp.int32, (BLK, BLK), 0)
        <= lax.broadcasted_iota(jnp.int32, (BLK, BLK), 1)
    ).astype(F32)
    heads, length = ld_ref.shape
    for b in range(length // BLK):
        span = slice(b * BLK, (b + 1) * BLK)
        sums = LOG2E * jnp.dot(
            ld_ref[:, span], upper, precision=lax.Precision.HIGHEST, preferred_element_type=F32
        )
        grown = jnp.exp2(sums)
        left = jnp.exp2(sums[:, BLK - 1 : BLK] - sums)
        for i in range(heads // 2):
            pair = slice(2 * i, 2 * i + 2)
            rows[i, :, span] = jnp.concatenate(
                [sums[pair], grown[pair], left[pair], sums[pair] - 7.0], axis=0
            )


def down(row):
    return jnp.broadcast_to(row, (LANES, LANES)).T


def diagonal(a, b):
    zero = jnp.zeros_like(a)
    return jnp.concatenate(
        [jnp.concatenate([a, zero], axis=1), jnp.concatenate([zero, b], axis=1)], axis=0
    )


def prepare_kernel(
    remote, q_any, k_any, v_any, ld_any, w_any, halo, rows, taps, ld, send_sem, recv_sem, local_sem
):
    length = q_any.shape[1]
    local = [
        pltpu.make_async_copy(ld_any, ld, local_sem.at[0]),
        pltpu.make_async_copy(w_any, taps, local_sem.at[1]),
    ]
    for copy in local:
        copy.start()
    copies = []
    if remote:
        other = {"ctx": 1 - lax.axis_index("ctx")}
        barrier = pltpu.get_barrier_semaphore()
        pl.semaphore_signal(barrier, inc=1, device_id=other, device_id_type=MESH)
        pl.semaphore_wait(barrier, 1)
        copies = [
            pltpu.make_async_remote_copy(
                src_ref=source.at[0, pl.ds(length - RIM, RIM), :],
                dst_ref=halo.at[m],
                send_sem=send_sem.at[m],
                recv_sem=recv_sem.at[m],
                device_id=other,
                device_id_type=MESH,
            )
            for m, source in enumerate((q_any, k_any, v_any))
        ]
    else:
        halo[...] = jnp.zeros_like(halo)
    for copy in copies:
        copy.start()
    local[0].wait()
    decay_tables(ld, rows)
    local[1].wait()
    for copy in copies:
        copy.wait()


def prepare(query, key, value, log_decay, conv_kernel, remote):
    _, length, width = query.shape
    heads = log_decay.shape[0]
    anywhere = pl.BlockSpec(memory_space=pl.ANY)
    vmem = pl.BlockSpec(memory_space=pltpu.VMEM)
    dma = pltpu.SemaphoreType.DMA
    inputs = (query, key, value, log_decay, conv_kernel)
    return pl.pallas_call(
        functools.partial(prepare_kernel, remote),
        in_specs=[anywhere] * 5,
        out_specs=[vmem] * 3,
        out_shape=[
            pltpu.VMEM((3, RIM, width), BF16),
            pltpu.VMEM((heads // 2, 8, length), F32),
            pltpu.VMEM(conv_kernel.shape, F32),
        ],
        scratch_shapes=[pltpu.VMEM((heads, length), F32), dma((3,)), dma((3,)), dma((2,))],
        compiler_params=pltpu.CompilerParams(
            collective_id=0 if remote else None, has_side_effects=True
        ),
        name="prepare",
    )(*(pltpu.with_memory_space_constraint(x, pltpu.HBM) for x in inputs))


def main_kernel(
    remote,
    q_any, k_any, v_any, g_any, halo_ref, rows, w_ref,
    store, kernel_grad_ref,
    xs, scaled, s_first, f_last, msg_out, msg_in, rim_out, rim_in,
    terms, pieces, landed, part_out, part_in,
    in_sem, msg_send, msg_recv, rim_send, rim_recv, piece_send, piece_recv, part_send,
    part_recv,
):
    steps, _, length, _ = store.shape
    core = lax.axis_index("ctx") if remote else 0
    dp = lax.axis_index("dp") if remote else 0
    peers = pieces.shape[0]
    other = {"ctx": 1 - core}
    share = (terms.shape[1] - LANES) // peers

    def columns(i, h=0, width=PAIR):
        return pl.ds(pl.multiple_of(i * PAIR + h * LANES, LANES), width)

    def fetch(i, m):
        source = (q_any, k_any, v_any, g_any)[m]
        return pltpu.make_async_copy(source.at[0, :, columns(i)], store.at[i, m], in_sem.at[i, m])

    def remote_copy(source, target, send_sem, recv_sem, device):
        return pltpu.make_async_remote_copy(
            src_ref=source, dst_ref=target, send_sem=send_sem, recv_sem=recv_sem,
            device_id=device, device_id_type=MESH,
        )

    state_spans = ((0, 2), (2, steps - 2), (steps - 2, steps))
    rim_spans = ((0, steps // 2), (steps // 2, steps))

    def state_copy(n):
        low, high = state_spans[n]
        span = pl.ds(2 * low, 2 * (high - low))
        return remote_copy(msg_out.at[span], msg_in.at[span], msg_send.at[n], msg_recv.at[n], other)

    def rim_copy(n):
        low, high = rim_spans[n]
        span = pl.ds(low, high - low)
        return remote_copy(rim_out.at[span], rim_in.at[span], rim_send.at[n], rim_recv.at[n], other)

    def loop(count, body):
        def step(i, carry):
            body(i)
            return carry

        lax.fori_loop(0, count, step, 0)

    @functools.partial(loop, steps)
    def _(i):
        for m in range(4):
            fetch(i, m).start()

    if remote:
        barrier = pltpu.get_barrier_semaphore()
        pl.semaphore_signal(barrier, inc=1, device_id=other, device_id_type=MESH)

        @functools.partial(loop, peers - 1)
        def _(d):
            peer = {"dp": lax.rem(dp + d + 1, peers)}
            pl.semaphore_signal(barrier, inc=1, device_id=peer, device_id_type=MESH)
    else:
        msg_in[...] = jnp.zeros_like(msg_in)

    first, last = pl.ds(0, BLK), pl.ds(BLK, BLK)

    def states(i):
        table = rows[i]
        state = dot(store[i, 1, first, :], scaled[2, i, first, :], TN)
        future = dot(store[i, 0, last, :], scaled[0, i, last, :], TN)
        message = dot(
            jnp.where(core == 0, store[i, 1, last, :], store[i, 0, first, :]),
            jnp.where(core == 0, scaled[2, i, last, :], scaled[0, i, first, :]),
            TN,
        )
        for h in range(2):
            c = slice(h * LANES, (h + 1) * LANES)
            decay = [table[2 + h : 3 + h, (b + 1) * BLK - 1 : (b + 1) * BLK] for b in range(2)]
            s_first[2 * i + h] = state[c, c]
            f_last[2 * i + h] = future[c, c]
            msg_out[2 * i + h] = (
                message[c, c]
                + jnp.where(core == 0, decay[1] * state[c, c], decay[0] * future[c, c])
            ).astype(BF16)

    def first_piece(i):
        return 16 * (i // 3) + 5 * lax.rem(i, 3)

    def piece_count(i):
        return jnp.where(lax.rem(i, 3) == 2, 6, 5)

    def pack(i):
        part = lax.rem(i, 3)
        base = 3 * PAIR * (i // 3) + jnp.where(part == 0, 0, jnp.where(part == 1, 128, 384))
        shift = jnp.where(part == 0, 0, jnp.where(part == 1, 512 - 112, 512 - 96))
        window = pltpu.roll(terms[:, pl.ds(pl.multiple_of(base, LANES), 512)], shift, 1)
        for n in range(6):
            piece = window[:, n * share : n * share + 64]
            pieces[first_piece(i) + n] = jnp.concatenate([piece[:8], piece[8:]], axis=1)

    def send(i, count):
        @functools.partial(loop, count)
        def _(n):
            owner = first_piece(i) + n

            @pl.when(owner != dp)
            def _():
                slot = lax.rem(dp - owner + peers, peers)
                remote_copy(
                    pieces.at[owner], landed.at[slot], piece_send, piece_recv, {"dp": owner}
                ).start()

    def spread(i, h, low, high):
        c = slice(h * LANES, (h + 1) * LANES)
        for m in range(3):
            taps = [w_ref[m, j : j + 1, columns(i, h, LANES)] for j in range(4)]
            for r in range(low, high, CHUNK):
                size = min(CHUNK, high - r)
                at = RIM + r
                acc = taps[0] * xs[i, h, m, at : at + size]
                for j in range(1, 4):
                    acc = acc + taps[j] * xs[i, h, m, at + j : at + j + size]
                store[i, m, r : r + size, c] = acc.astype(BF16)

    @functools.partial(loop, steps)
    def _(i):
        for m in range(4):
            fetch(i, m).wait()
        if remote:

            @pl.when(i == steps - 1)
            def _():
                pl.semaphore_wait(pltpu.get_barrier_semaphore(), peers)
                state_copy(0).start()
                state_copy(1).start()

        table = rows[i]
        for h in range(2):
            c = slice(h * LANES, (h + 1) * LANES)
            if h == 1:
                states(jnp.maximum(i - 1, 0))
            for m in range(3):
                before = halo_ref[m, :, columns(i, h, LANES)].astype(F32)
                xs[i, h, m, 0:RIM] = jnp.where(core == 1, before, 0.0)
                for r in range(0, length, CHUNK):
                    xs[i, h, m, RIM + r : RIM + r + CHUNK] = store[i, m, r : r + CHUNK, c].astype(F32)
            taps = [[w_ref[m, j : j + 1, columns(i, h, LANES)] for j in range(4)] for m in range(3)]
            for base in range(0, length, LANES):
                grown = down(table[2 + h : 3 + h, base : base + LANES])
                left = down(table[4 + h : 5 + h, base : base + LANES])
                for r in range(0, LANES, CHUNK):
                    part = slice(base + r, base + r + CHUNK)
                    near = slice(r, r + CHUNK)
                    for m in range(3):
                        at = RIM + base + r
                        acc = taps[m][0] * xs[i, h, m, at : at + CHUNK]
                        for j in range(1, 4):
                            acc = acc + taps[m][j] * xs[i, h, m, at - j : at - j + CHUNK]
                        store[i, m, part, c] = acc.astype(BF16)
                        if m > 0:
                            scaled[m, i, part, c] = (acc * left[near]).astype(BF16)
                    scaled[0, i, part, c] = (store[i, 3, part, c].astype(F32) * grown[near]).astype(BF16)

    states(steps - 1)
    if remote:
        state_copy(2).start()

    @functools.partial(loop, steps)
    def _(i):
        if remote:
            for n, (low, _) in enumerate(state_spans):

                @pl.when(i == low)
                def _():
                    state_copy(n).wait()

        pack(jnp.maximum(i - 1, 0))
        table = rows[i]
        scale = 1.0 / LANES
        causal = lax.broadcasted_iota(jnp.int32, (HALF, HALF), 0) <= lax.broadcasted_iota(
            jnp.int32, (HALF, HALF), 1
        )
        blank = jnp.zeros((HALF, HALF), BF16)
        incoming, future = [], []
        for h in range(2):
            decay = [table[2 + h : 3 + h, (b + 1) * BLK - 1 : (b + 1) * BLK] for b in range(2)]
            message = msg_in[2 * i + h].astype(F32) * scale
            state_in = jnp.where(core == 1, message, 0.0)
            future_in = jnp.where(core == 0, message, 0.0)
            state = decay[0] * state_in + scale * s_first[2 * i + h]
            grads = decay[1] * future_in + scale * f_last[2 * i + h]
            incoming.append([state_in.astype(BF16), state.astype(BF16)])
            future.append([grads.astype(BF16), future_in.astype(BF16)])
        kernel_sums = [[[jnp.zeros((8, LANES), F32)] * 4 for _ in range(3)] for _ in range(2)]
        for h in range(2):
            c = slice(h * LANES, (h + 1) * LANES)
            for b in (1, 0):
                part = slice(b * BLK, (b + 1) * BLK)
                q, k, v, g = (store[i, m, part, c] for m in range(4))
                row = table[h : h + 1, part]
                lowered = table[6 + h : 7 + h, part]

                def weight(s, t):
                    mine = jnp.exp2(
                        lowered[:, t * HALF : (t + 1) * HALF]
                        - down(row[:, s * HALF : (s + 1) * HALF])
                    )
                    return jnp.where(causal, mine, 0.0) if s == t else mine

                top = jnp.concatenate([weight(0, 0), weight(0, 1)], axis=1)
                low = weight(1, 1)

                def masked(full):
                    upper = (full[:HALF] * top).astype(BF16)
                    lower = (full[HALF:, HALF:] * low).astype(BF16)
                    return jnp.concatenate(
                        [upper, jnp.concatenate([blank, lower], axis=1)], axis=0
                    )

                gt = masked(dot(v, g, NT))
                pt = masked(dot(k, q, NT))
                wg, wk, wv = (scaled[m, i, part, c] for m in range(3))
                before, after = incoming[h][b], future[h][b]
                grads = (
                    dot(gt, k, TN) + dot(wg, before, NT),
                    dot(gt, q, NN) + dot(wv, after, NT),
                    dot(pt, g, NN) + dot(wk, after, NN),
                )
                for m in range(3):
                    for half in (1, 0):
                        at = RIM + b * BLK + half * HALF
                        mine = grads[m][half * HALF : (half + 1) * HALF]
                        for j in range(4):
                            product = xs[i, h, m, at - j : at - j + HALF] * mine
                            kernel_sums[h][m][j] = kernel_sums[h][m][j] + jnp.sum(
                                product.reshape(HALF // 8, 8, LANES), axis=0
                            )
                        xs[i, h, m, at : at + HALF] = mine
        for h in range(2):
            sums = [
                jnp.sum(kernel_sums[h][m][j], axis=0, keepdims=True)
                for m in range(3)
                for j in range(4)
            ]
            terms[:, columns(i, h, LANES)] = jnp.concatenate(
                sums + [jnp.zeros((4, LANES), F32)], axis=0
            )
        for h in range(2):
            for m in range(3):
                rim_out[i, h, m] = xs[i, h, m, RIM : RIM + 8]
        if remote:
            for n, (_, high) in enumerate(rim_spans):

                @pl.when(i == high - 1)
                def _():
                    rim_copy(n).start()

        if remote:
            send(i - 1, jnp.where(i == 0, 0, piece_count(i - 1)))

    pack(steps - 1)
    if remote:
        send(steps - 1, piece_count(steps - 1))

    @functools.partial(loop, steps)
    def _(i):
        spread(i, 0, 0, length - RIM)
        spread(i, 1, 0, length - RIM)

    if remote:
        for n in range(len(rim_spans)):
            rim_copy(n).wait()

    @functools.partial(loop, steps)
    def _(i):
        tail = slice(RIM + length, RIM + length + 8)
        for h in range(2):
            for m in range(3):
                xs[i, h, m, tail] = jnp.where(core == 0, rim_in[i, h, m], 0.0)
            spread(i, h, length - RIM, length)

    if remote:
        others = pl.ds(1, peers - 1)
        remote_copy(pieces.at[others], landed.at[others], piece_send, piece_recv, other).wait()
        total = pieces[dp] + jnp.sum(landed[1:], axis=0)
        part_out[...] = total
        copy = remote_copy(part_out, part_in, part_send, part_recv, other)
        copy.start()
        copy.wait()
        total = (total + part_in[...]) * (1.0 / peers)
    else:
        total = pieces[dp]
    kernel_grad_ref[0] = total[0:4, :share]
    kernel_grad_ref[1] = total[4:8, :share]
    kernel_grad_ref[2] = total[0:4, 64 : 64 + share]


def gradients(query, key, value, out_grad, log_decay, conv_kernel, remote=True):
    _, length, width = query.shape
    heads = log_decay.shape[1]
    steps = width // PAIR
    peers = lax.axis_size("dp") if remote else 64
    dma = pltpu.SemaphoreType.DMA
    anywhere = pl.BlockSpec(memory_space=pl.ANY)
    vmem = pl.BlockSpec(memory_space=pltpu.VMEM)
    prepared = prepare(query, key, value, log_decay[0], conv_kernel, remote)
    prepared = [pltpu.with_memory_space_constraint(x, pltpu.VMEM) for x in prepared]
    return pl.pallas_call(
        functools.partial(main_kernel, remote),
        in_specs=[anywhere] * 4 + [vmem] * 3,
        out_specs=[vmem, vmem],
        out_shape=[
            pltpu.VMEM((steps, 4, length, PAIR), BF16),
            pltpu.VMEM((3, 4, width // peers), F32),
        ],
        scratch_shapes=[
            pltpu.VMEM((steps, 2, 3, RIM + length + 8, LANES), F32),
            pltpu.VMEM((3, steps, length, PAIR), BF16),
            pltpu.VMEM((heads, LANES, LANES), F32),
            pltpu.VMEM((heads, LANES, LANES), F32),
            pltpu.VMEM((heads, LANES, LANES), BF16),
            pltpu.VMEM((heads, LANES, LANES), BF16),
            pltpu.VMEM((steps, 2, 3, 8, LANES), F32),
            pltpu.VMEM((steps, 2, 3, 8, LANES), F32),
            pltpu.VMEM((16, width + LANES), F32),
            pltpu.VMEM((peers, 8, LANES), F32),
            pltpu.VMEM((peers, 8, LANES), F32),
            pltpu.VMEM((8, LANES), F32),
            pltpu.VMEM((8, LANES), F32),
            dma((steps, 4)),
            dma((3,)), dma((3,)), dma((2,)), dma((2,)),
            dma, dma, dma, dma,
        ],
        compiler_params=pltpu.CompilerParams(
            collective_id=1 if remote else None,
            has_side_effects=True,
            vmem_limit_bytes=46 * 1024 * 1024,
        ),
        name="gradients",
    )(
        *(pltpu.with_memory_space_constraint(x, pltpu.HBM) for x in (query, key, value, out_grad)),
        *prepared,
    )


def flush_kernel(store, kernel_grad_in, oq_any, ok_any, ov_any, kernel_grad_out, sem, last_sem):
    steps = store.shape[0]
    copies = [pltpu.make_async_copy(kernel_grad_in, kernel_grad_out, last_sem)] + [
        pltpu.make_async_copy(
            store.at[i, m], out.at[0, :, pl.ds(i * PAIR, PAIR)], sem.at[i, m]
        )
        for i in range(steps)
        for m, out in enumerate((oq_any, ok_any, ov_any))
    ]
    for copy in copies:
        copy.start()
    for copy in copies:
        copy.wait()


def flush(store, kernel_grad):
    steps, _, length, _ = store.shape
    anywhere = pl.BlockSpec(memory_space=pl.ANY)
    vmem = pl.BlockSpec(memory_space=pltpu.VMEM)
    return pl.pallas_call(
        flush_kernel,
        in_specs=[vmem, vmem],
        out_specs=[anywhere] * 4,
        out_shape=[jax.ShapeDtypeStruct((1, length, steps * PAIR), BF16)] * 3
        + [jax.ShapeDtypeStruct(kernel_grad.shape, F32)],
        scratch_shapes=[pltpu.SemaphoreType.DMA((steps, 3)), pltpu.SemaphoreType.DMA],
        compiler_params=pltpu.CompilerParams(vmem_limit_bytes=16 * 1024 * 1024),
        name="flush",
    )(*(pltpu.with_memory_space_constraint(x, pltpu.VMEM) for x in (store, kernel_grad)))


def local(query, key, value, out_grad, log_decay, conv_kernel):
    store, kernel_grad = gradients(query, key, value, out_grad, log_decay, conv_kernel)
    return tuple(flush(store, kernel_grad))


def solution(mesh):
    rows = P("dp", "ctx", None)
    return jax.shard_map(
        local,
        mesh=mesh,
        in_specs=(rows, rows, rows, rows, P("dp", None, "ctx"), P()),
        out_specs=(rows, rows, rows, P(None, None, "dp")),
        check_vma=False,
    )
```

```python
import functools

import jax
import jax.numpy as jnp
from jax import lax
from jax.experimental import pallas as pl
from jax.experimental.pallas import tpu as pltpu
from jax.sharding import PartitionSpec as P

MESH = pl.DeviceIdType.MESH
BLK = 256
HALF = 128
LANES = 128
PAIR = 256
RIM = 16
CHUNK = 64
LOG2E = 1.4426950408889634
F32 = jnp.float32
BF16 = jnp.bfloat16
NT = (((1,), (1,)), ((), ()))
TN = (((0,), (0,)), ((), ()))
NN = (((1,), (0,)), ((), ()))


def dot(a, b, dims):
    return lax.dot_general(a, b, dims, preferred_element_type=F32)


def decay_tables(ld_ref, rows):
    upper = (
        lax.broadcasted_iota(jnp.int32, (BLK, BLK), 0)
        <= lax.broadcasted_iota(jnp.int32, (BLK, BLK), 1)
    ).astype(F32)
    heads, length = ld_ref.shape
    for b in range(length // BLK):
        span = slice(b * BLK, (b + 1) * BLK)
        sums = LOG2E * jnp.dot(
            ld_ref[:, span], upper, precision=lax.Precision.HIGHEST, preferred_element_type=F32
        )
        grown = jnp.exp2(sums)
        left = jnp.exp2(sums[:, BLK - 1 : BLK] - sums)
        for i in range(heads // 2):
            pair = slice(2 * i, 2 * i + 2)
            rows[i, :, span] = jnp.concatenate(
                [sums[pair], grown[pair], left[pair], sums[pair] - 7.0], axis=0
            )


def down(row):
    return jnp.broadcast_to(row, (LANES, LANES)).T


def diagonal(a, b):
    zero = jnp.zeros_like(a)
    return jnp.concatenate(
        [jnp.concatenate([a, zero], axis=1), jnp.concatenate([zero, b], axis=1)], axis=0
    )


def prepare_kernel(
    remote, q_any, k_any, v_any, ld_any, w_any, halo, rows, taps, ld, send_sem, recv_sem, local_sem
):
    length = q_any.shape[1]
    local = [
        pltpu.make_async_copy(ld_any, ld, local_sem.at[0]),
        pltpu.make_async_copy(w_any, taps, local_sem.at[1]),
    ]
    for copy in local:
        copy.start()
    copies = []
    if remote:
        other = {"ctx": 1 - lax.axis_index("ctx")}
        barrier = pltpu.get_barrier_semaphore()
        pl.semaphore_signal(barrier, inc=1, device_id=other, device_id_type=MESH)
        pl.semaphore_wait(barrier, 1)
        copies = [
            pltpu.make_async_remote_copy(
                src_ref=source.at[0, pl.ds(length - RIM, RIM), :],
                dst_ref=halo.at[m],
                send_sem=send_sem.at[m],
                recv_sem=recv_sem.at[m],
                device_id=other,
                device_id_type=MESH,
            )
            for m, source in enumerate((q_any, k_any, v_any))
        ]
    else:
        halo[...] = jnp.zeros_like(halo)
    for copy in copies:
        copy.start()
    local[0].wait()
    decay_tables(ld, rows)
    local[1].wait()
    for copy in copies:
        copy.wait()


def prepare(query, key, value, log_decay, conv_kernel, remote):
    _, length, width = query.shape
    heads = log_decay.shape[0]
    anywhere = pl.BlockSpec(memory_space=pl.ANY)
    vmem = pl.BlockSpec(memory_space=pltpu.VMEM)
    dma = pltpu.SemaphoreType.DMA
    inputs = (query, key, value, log_decay, conv_kernel)
    return pl.pallas_call(
        functools.partial(prepare_kernel, remote),
        in_specs=[anywhere] * 5,
        out_specs=[vmem] * 3,
        out_shape=[
            pltpu.VMEM((3, RIM, width), BF16),
            pltpu.VMEM((heads // 2, 8, length), F32),
            pltpu.VMEM(conv_kernel.shape, F32),
        ],
        scratch_shapes=[pltpu.VMEM((heads, length), F32), dma((3,)), dma((3,)), dma((2,))],
        compiler_params=pltpu.CompilerParams(
            collective_id=0 if remote else None, has_side_effects=True
        ),
        name="prepare",
    )(*(pltpu.with_memory_space_constraint(x, pltpu.HBM) for x in inputs))


def main_kernel(
    remote,
    q_any, k_any, v_any, g_any, halo_ref, rows, w_ref,
    store, kernel_grad_ref,
    xs, scaled, s_first, f_last, msg_out, msg_in, rim_out, rim_in,
    terms, pieces, landed, part_out, part_in,
    in_sem, msg_send, msg_recv, rim_send, rim_recv, piece_send, piece_recv, part_send,
    part_recv,
):
    steps, _, length, _ = store.shape
    core = lax.axis_index("ctx") if remote else 0
    dp = lax.axis_index("dp") if remote else 0
    peers = pieces.shape[0]
    other = {"ctx": 1 - core}
    share = (terms.shape[1] - LANES) // peers

    def columns(i, h=0, width=PAIR):
        return pl.ds(pl.multiple_of(i * PAIR + h * LANES, LANES), width)

    def fetch(i, m):
        source = (q_any, k_any, v_any, g_any)[m]
        return pltpu.make_async_copy(source.at[0, :, columns(i)], store.at[i, m], in_sem.at[i, m])

    def remote_copy(source, target, send_sem, recv_sem, device):
        return pltpu.make_async_remote_copy(
            src_ref=source, dst_ref=target, send_sem=send_sem, recv_sem=recv_sem,
            device_id=device, device_id_type=MESH,
        )

    state_spans = ((0, 2), (2, steps - 2), (steps - 2, steps))
    rim_spans = ((0, steps // 2), (steps // 2, steps))

    def state_copy(n):
        low, high = state_spans[n]
        span = pl.ds(2 * low, 2 * (high - low))
        return remote_copy(msg_out.at[span], msg_in.at[span], msg_send.at[n], msg_recv.at[n], other)

    def rim_copy(n):
        low, high = rim_spans[n]
        span = pl.ds(low, high - low)
        return remote_copy(rim_out.at[span], rim_in.at[span], rim_send.at[n], rim_recv.at[n], other)

    def loop(count, body):
        def step(i, carry):
            body(i)
            return carry

        lax.fori_loop(0, count, step, 0)

    @functools.partial(loop, steps)
    def _(i):
        for m in range(4):
            fetch(i, m).start()

    if remote:
        barrier = pltpu.get_barrier_semaphore()
        pl.semaphore_signal(barrier, inc=1, device_id=other, device_id_type=MESH)

        @functools.partial(loop, peers - 1)
        def _(d):
            peer = {"dp": lax.rem(dp + d + 1, peers)}
            pl.semaphore_signal(barrier, inc=1, device_id=peer, device_id_type=MESH)
    else:
        msg_in[...] = jnp.zeros_like(msg_in)

    first, last = pl.ds(0, BLK), pl.ds(BLK, BLK)

    def states(i):
        table = rows[i]
        state = dot(store[i, 1, first, :], scaled[2, i, first, :], TN)
        future = dot(store[i, 0, last, :], scaled[0, i, last, :], TN)
        message = dot(
            jnp.where(core == 0, store[i, 1, last, :], store[i, 0, first, :]),
            jnp.where(core == 0, scaled[2, i, last, :], scaled[0, i, first, :]),
            TN,
        )
        for h in range(2):
            c = slice(h * LANES, (h + 1) * LANES)
            decay = [table[2 + h : 3 + h, (b + 1) * BLK - 1 : (b + 1) * BLK] for b in range(2)]
            s_first[2 * i + h] = state[c, c]
            f_last[2 * i + h] = future[c, c]
            msg_out[2 * i + h] = (
                message[c, c]
                + jnp.where(core == 0, decay[1] * state[c, c], decay[0] * future[c, c])
            ).astype(BF16)

    def first_piece(i):
        return 16 * (i // 3) + 5 * lax.rem(i, 3)

    def piece_count(i):
        return jnp.where(lax.rem(i, 3) == 2, 6, 5)

    def pack(i):
        part = lax.rem(i, 3)
        base = 3 * PAIR * (i // 3) + jnp.where(part == 0, 0, jnp.where(part == 1, 128, 384))
        shift = jnp.where(part == 0, 0, jnp.where(part == 1, 512 - 112, 512 - 96))
        window = pltpu.roll(terms[:, pl.ds(pl.multiple_of(base, LANES), 512)], shift, 1)
        for n in range(6):
            piece = window[:, n * share : n * share + 64]
            pieces[first_piece(i) + n] = jnp.concatenate([piece[:8], piece[8:]], axis=1)

    def send(i, count):
        @functools.partial(loop, count)
        def _(n):
            owner = first_piece(i) + n

            @pl.when(owner != dp)
            def _():
                slot = lax.rem(dp - owner + peers, peers)
                remote_copy(
                    pieces.at[owner], landed.at[slot], piece_send, piece_recv, {"dp": owner}
                ).start()

    def spread(i, h, low, high):
        c = slice(h * LANES, (h + 1) * LANES)
        for m in range(3):
            taps = [w_ref[m, j : j + 1, columns(i, h, LANES)] for j in range(4)]
            for r in range(low, high, CHUNK):
                size = min(CHUNK, high - r)
                at = RIM + r
                acc = taps[0] * xs[i, h, m, at : at + size]
                for j in range(1, 4):
                    acc = acc + taps[j] * xs[i, h, m, at + j : at + j + size]
                store[i, m, r : r + size, c] = acc.astype(BF16)

    @functools.partial(loop, steps)
    def _(i):
        for m in range(4):
            fetch(i, m).wait()
        if remote:

            @pl.when(i == steps - 1)
            def _():
                pl.semaphore_wait(pltpu.get_barrier_semaphore(), peers)
                state_copy(0).start()
                state_copy(1).start()

        table = rows[i]
        for h in range(2):
            c = slice(h * LANES, (h + 1) * LANES)
            if h == 1:
                states(jnp.maximum(i - 1, 0))
            for m in range(3):
                before = halo_ref[m, :, columns(i, h, LANES)].astype(F32)
                xs[i, h, m, 0:RIM] = jnp.where(core == 1, before, 0.0)
                for r in range(0, length, CHUNK):
                    xs[i, h, m, RIM + r : RIM + r + CHUNK] = store[i, m, r : r + CHUNK, c].astype(F32)
            taps = [[w_ref[m, j : j + 1, columns(i, h, LANES)] for j in range(4)] for m in range(3)]
            for base in range(0, length, LANES):
                grown = down(table[2 + h : 3 + h, base : base + LANES])
                left = down(table[4 + h : 5 + h, base : base + LANES])
                for r in range(0, LANES, CHUNK):
                    part = slice(base + r, base + r + CHUNK)
                    near = slice(r, r + CHUNK)
                    for m in range(3):
                        at = RIM + base + r
                        acc = taps[m][0] * xs[i, h, m, at : at + CHUNK]
                        for j in range(1, 4):
                            acc = acc + taps[m][j] * xs[i, h, m, at - j : at - j + CHUNK]
                        store[i, m, part, c] = acc.astype(BF16)
                        if m > 0:
                            scaled[m, i, part, c] = (acc * left[near]).astype(BF16)
                    scaled[0, i, part, c] = (store[i, 3, part, c].astype(F32) * grown[near]).astype(BF16)

    states(steps - 1)
    if remote:
        state_copy(2).start()

    @functools.partial(loop, steps)
    def _(i):
        if remote:
            for n, (low, _) in enumerate(state_spans):

                @pl.when(i == low)
                def _():
                    state_copy(n).wait()

        pack(jnp.maximum(i - 1, 0))
        table = rows[i]
        scale = 1.0 / LANES
        causal = lax.broadcasted_iota(jnp.int32, (HALF, HALF), 0) <= lax.broadcasted_iota(
            jnp.int32, (HALF, HALF), 1
        )
        blank = jnp.zeros((HALF, HALF), BF16)
        incoming, future = [], []
        for h in range(2):
            decay = [table[2 + h : 3 + h, (b + 1) * BLK - 1 : (b + 1) * BLK] for b in range(2)]
            message = msg_in[2 * i + h].astype(F32) * scale
            state_in = jnp.where(core == 1, message, 0.0)
            future_in = jnp.where(core == 0, message, 0.0)
            state = decay[0] * state_in + scale * s_first[2 * i + h]
            grads = decay[1] * future_in + scale * f_last[2 * i + h]
            incoming.append([state_in.astype(BF16), state.astype(BF16)])
            future.append([grads.astype(BF16), future_in.astype(BF16)])
        kernel_sums = [[[jnp.zeros((8, LANES), F32)] * 4 for _ in range(3)] for _ in range(2)]
        for h in range(2):
            c = slice(h * LANES, (h + 1) * LANES)
            for b in (1, 0):
                part = slice(b * BLK, (b + 1) * BLK)
                q, k, v, g = (store[i, m, part, c] for m in range(4))
                row = table[h : h + 1, part]
                lowered = table[6 + h : 7 + h, part]

                def weight(s, t):
                    mine = jnp.exp2(
                        lowered[:, t * HALF : (t + 1) * HALF]
                        - down(row[:, s * HALF : (s + 1) * HALF])
                    )
                    return jnp.where(causal, mine, 0.0) if s == t else mine

                top = jnp.concatenate([weight(0, 0), weight(0, 1)], axis=1)
                low = weight(1, 1)

                def masked(full):
                    upper = (full[:HALF] * top).astype(BF16)
                    lower = (full[HALF:, HALF:] * low).astype(BF16)
                    return jnp.concatenate(
                        [upper, jnp.concatenate([blank, lower], axis=1)], axis=0
                    )

                gt = masked(dot(v, g, NT))
                pt = masked(dot(k, q, NT))
                wg, wk, wv = (scaled[m, i, part, c] for m in range(3))
                before, after = incoming[h][b], future[h][b]
                grads = (
                    dot(gt, k, TN) + dot(wg, before, NT),
                    dot(gt, q, NN) + dot(wv, after, NT),
                    dot(pt, g, NN) + dot(wk, after, NN),
                )
                for m in range(3):
                    for half in (1, 0):
                        at = RIM + b * BLK + half * HALF
                        mine = grads[m][half * HALF : (half + 1) * HALF]
                        for j in range(4):
                            product = xs[i, h, m, at - j : at - j + HALF] * mine
                            kernel_sums[h][m][j] = kernel_sums[h][m][j] + jnp.sum(
                                product.reshape(HALF // 8, 8, LANES), axis=0
                            )
                        xs[i, h, m, at : at + HALF] = mine
        for h in range(2):
            sums = [
                jnp.sum(kernel_sums[h][m][j], axis=0, keepdims=True)
                for m in range(3)
                for j in range(4)
            ]
            terms[:, columns(i, h, LANES)] = jnp.concatenate(
                sums + [jnp.zeros((4, LANES), F32)], axis=0
            )
        for h in range(2):
            for m in range(3):
                rim_out[i, h, m] = xs[i, h, m, RIM : RIM + 8]
        if remote:
            for n, (_, high) in enumerate(rim_spans):

                @pl.when(i == high - 1)
                def _():
                    rim_copy(n).start()

        if remote:
            send(i - 1, jnp.where(i == 0, 0, piece_count(i - 1)))

    pack(steps - 1)
    if remote:
        send(steps - 1, piece_count(steps - 1))

    @functools.partial(loop, steps)
    def _(i):
        spread(i, 0, 0, length - RIM)
        spread(i, 1, 0, length - RIM)

    if remote:
        for n in range(len(rim_spans)):
            rim_copy(n).wait()

    for i in range(steps):
        tail = slice(RIM + length, RIM + length + 8)
        for h in range(2):
            for m in range(3):
                xs[i, h, m, tail] = jnp.where(core == 0, rim_in[i, h, m], 0.0)
            spread(i, h, length - RIM, length)

    if remote:
        others = pl.ds(1, peers - 1)
        remote_copy(pieces.at[others], landed.at[others], piece_send, piece_recv, other).wait()
        total = pieces[dp] + jnp.sum(landed[1:], axis=0)
        part_out[...] = total
        copy = remote_copy(part_out, part_in, part_send, part_recv, other)
        copy.start()
        copy.wait()
        total = (total + part_in[...]) * (1.0 / peers)
    else:
        total = pieces[dp]
    kernel_grad_ref[0] = total[0:4, :share]
    kernel_grad_ref[1] = total[4:8, :share]
    kernel_grad_ref[2] = total[0:4, 64 : 64 + share]


def gradients(query, key, value, out_grad, log_decay, conv_kernel, remote=True):
    _, length, width = query.shape
    heads = log_decay.shape[1]
    steps = width // PAIR
    peers = lax.axis_size("dp") if remote else 64
    dma = pltpu.SemaphoreType.DMA
    anywhere = pl.BlockSpec(memory_space=pl.ANY)
    vmem = pl.BlockSpec(memory_space=pltpu.VMEM)
    prepared = prepare(query, key, value, log_decay[0], conv_kernel, remote)
    prepared = [pltpu.with_memory_space_constraint(x, pltpu.VMEM) for x in prepared]
    return pl.pallas_call(
        functools.partial(main_kernel, remote),
        in_specs=[anywhere] * 4 + [vmem] * 3,
        out_specs=[vmem, vmem],
        out_shape=[
            pltpu.VMEM((steps, 4, length, PAIR), BF16),
            pltpu.VMEM((3, 4, width // peers), F32),
        ],
        scratch_shapes=[
            pltpu.VMEM((steps, 2, 3, RIM + length + 8, LANES), F32),
            pltpu.VMEM((3, steps, length, PAIR), BF16),
            pltpu.VMEM((heads, LANES, LANES), F32),
            pltpu.VMEM((heads, LANES, LANES), F32),
            pltpu.VMEM((heads, LANES, LANES), BF16),
            pltpu.VMEM((heads, LANES, LANES), BF16),
            pltpu.VMEM((steps, 2, 3, 8, LANES), F32),
            pltpu.VMEM((steps, 2, 3, 8, LANES), F32),
            pltpu.VMEM((16, width + LANES), F32),
            pltpu.VMEM((peers, 8, LANES), F32),
            pltpu.VMEM((peers, 8, LANES), F32),
            pltpu.VMEM((8, LANES), F32),
            pltpu.VMEM((8, LANES), F32),
            dma((steps, 4)),
            dma((3,)), dma((3,)), dma((2,)), dma((2,)),
            dma, dma, dma, dma,
        ],
        compiler_params=pltpu.CompilerParams(
            collective_id=1 if remote else None,
            has_side_effects=True,
            vmem_limit_bytes=46 * 1024 * 1024,
        ),
        name="gradients",
    )(
        *(pltpu.with_memory_space_constraint(x, pltpu.HBM) for x in (query, key, value, out_grad)),
        *prepared,
    )


def flush_kernel(store, kernel_grad_in, oq_any, ok_any, ov_any, kernel_grad_out, sem, last_sem):
    steps = store.shape[0]
    copies = [pltpu.make_async_copy(kernel_grad_in, kernel_grad_out, last_sem)] + [
        pltpu.make_async_copy(
            store.at[i, m], out.at[0, :, pl.ds(i * PAIR, PAIR)], sem.at[i, m]
        )
        for i in range(steps)
        for m, out in enumerate((oq_any, ok_any, ov_any))
    ]
    for copy in copies:
        copy.start()
    for copy in copies:
        copy.wait()


def flush(store, kernel_grad):
    steps, _, length, _ = store.shape
    anywhere = pl.BlockSpec(memory_space=pl.ANY)
    vmem = pl.BlockSpec(memory_space=pltpu.VMEM)
    return pl.pallas_call(
        flush_kernel,
        in_specs=[vmem, vmem],
        out_specs=[anywhere] * 4,
        out_shape=[jax.ShapeDtypeStruct((1, length, steps * PAIR), BF16)] * 3
        + [jax.ShapeDtypeStruct(kernel_grad.shape, F32)],
        scratch_shapes=[pltpu.SemaphoreType.DMA((steps, 3)), pltpu.SemaphoreType.DMA],
        compiler_params=pltpu.CompilerParams(vmem_limit_bytes=16 * 1024 * 1024),
        name="flush",
    )(*(pltpu.with_memory_space_constraint(x, pltpu.VMEM) for x in (store, kernel_grad)))


def local(query, key, value, out_grad, log_decay, conv_kernel):
    store, kernel_grad = gradients(query, key, value, out_grad, log_decay, conv_kernel)
    return tuple(flush(store, kernel_grad))


def solution(mesh):
    rows = P("dp", "ctx", None)
    return jax.shard_map(
        local,
        mesh=mesh,
        in_specs=(rows, rows, rows, rows, P("dp", None, "ctx"), P()),
        out_specs=(rows, rows, rows, P(None, None, "dp")),
        check_vma=False,
    )
```
